256 devices in a mesh: expert: 32 (over z_lo, y, x), mp: 8 (over z_hi, core).
Axes of the slice: x: 4, y: 4, z: 8 (z_hi: 4, z_lo: 2; z = z_hi * 2 + z_lo), core: 2. Of those that a mesh axis runs over, the one named last changes fastest.
Arguments:
- attention: bfloat16 [4096, 3584], P('expert', 'mp'), may hold values from -6 to 6
- out_weight: bfloat16 [3584, 7168], P('expert', 'mp'), may hold values from -0.09375 to 0.09375
- residual: bfloat16 [4096, 7168], P('expert', 'mp')
- norm_gain: float32 [7168], P('mp'), may hold values from 0.5 to 2
- expert_ids: int32 [4096, 2], P('expert'), may hold values from 0 to 15, as said below
- slot_index: int32 [4096, 2], P('expert'), may hold values from -1 to 19, as said below
- gate_prob: float32 [4096, 2], P('expert'), may hold values from 0.1 to 1
- w_gate: bfloat16 [32, 7168, 2048], P('expert', None, 'mp'), may hold values from -0.0625 to 0.0625
- w_up: bfloat16 [32, 7168, 2048], P('expert', None, 'mp'), may hold values from -0.0625 to 0.0625
- w_down: bfloat16 [32, 2048, 7168], P('expert', 'mp'), may hold values from -0.09375 to 0.09375
Outputs:
- layer_out: bfloat16 [4096, 7168], P('expert', 'mp')
The draws below stay inside these ranges and needn't reach their ends.
Inputs may be any that keep to these rules, and one draw needn't show every extreme that they name: `expert_ids`: each token names two different experts; in every block of 128 tokens some expert is named by more than 20 choices. `slot_index`: within each block of 128 tokens, the choices naming one expert take its slots 0, 1, 2, ... in order of token and then choice; those beyond its 20 slots get -1. Every block fills all slots of some expert.
All inputs are finite; a program needn't handle non-finite values.
Results may differ from the reference program's by a relative error of at most 0.0085.
Values may be sent and summed in bfloat16 or wider, within the bound.
No kernel may reach another device: no remote copies, remote signals or barrier semaphores. Data moves between devices by JAX's collectives and lax.ppermute only.
A program may use at most 128 MiB of HBM per device.

```python
import math
import jax
import jax.numpy as jnp
from jax import lax

D = 7168
HD = 3584
HID = 4096
TOK_DEV = 128
EXPERTS = 16
CAP = 20
TOKENS = 4096
N_MP = 8


def route_table(key):
    blocks = TOKENS // TOK_DEV
    first_key, pick_key, second_key = jax.random.split(key, 3)
    hottest = jax.random.randint(first_key, (blocks, 1), 0, EXPERTS)
    picks = jax.random.randint(pick_key, (blocks, TOK_DEV), 0, 4 * EXPERTS)
    first = jnp.where(picks < 3 * EXPERTS, picks % EXPERTS, hottest)
    offset = jax.random.randint(second_key, (blocks, TOK_DEV), 1, EXPERTS)
    second = (first + offset) % EXPERTS
    flattened = jnp.stack([first, second], axis=-1).reshape(blocks, 2 * TOK_DEV)
    onehot = (flattened[..., None] == jnp.arange(EXPERTS, dtype=jnp.int32)).astype(jnp.int32)
    ranks = jnp.cumsum(onehot, axis=1) - onehot
    placed = jnp.sum(ranks * onehot, axis=-1)
    slots_all = jnp.where(placed < CAP, placed, -1)
    return (flattened.reshape(TOKENS, 2).astype(jnp.int32), slots_all.reshape(TOKENS, 2).astype(jnp.int32))


def draw_expert_ids(key, part):
    chosen, placed = route_table(key)
    return chosen


def draw_slot_index(key, part):
    chosen, placed = route_table(key)
    return placed


def draw_residual(key, part):
    key = jax.random.fold_in(key, 7)
    column = jnp.arange(D, dtype=jnp.float32) / D
    scales = 0.4 * jnp.power(10.0, column)
    values = jax.random.truncated_normal(key, -4.0, 4.0, (TOKENS, D), jnp.float32) * scales
    return values.astype(jnp.bfloat16)


def levels(rng, dims, cuts, least, top_value):
    level = 1.0
    for position, shards_of in cuts:
        steps = jax.random.uniform(jax.random.fold_in(jax.random.fold_in(rng, 6), position), (shards_of,), jnp.float32, least / len(cuts), top_value / len(cuts))
        level = level * jnp.repeat(jnp.exp(steps), dims[position] // shards_of).reshape((-1,) + (1,) * (len(dims) - 1 - position))
    return level


def centred(stream_key, dims, scale, reach, shards=(), kind=jnp.bfloat16):
    loudness = levels(stream_key, dims, shards, -0.22, 0.18) if shards else 1.0
    values = jax.random.normal(stream_key, dims, jnp.float32) * scale * loudness
    return jnp.minimum(jnp.maximum(values, -reach), reach).astype(kind)


def setup_inputs(seed: int = 0) -> dict:
    streams_of = jax.random.split(jax.random.key(seed), 11)
    return {
        "attention": centred(streams_of[0], (TOKENS, HD), 1.0, 6.0, ((0, 32), (1, 8))),
        "out_weight": centred(streams_of[1], (HD, D), HD ** -0.5, 0.09375, ((0, 32), (1, 8))),
        "residual": draw_residual(jax.random.fold_in(streams_of[10], 71), 0),
        "norm_gain": jnp.clip(jnp.exp(math.log(2.0) - 1.3862944 * jax.random.uniform(streams_of[3], (D,), jnp.float32) ** levels(streams_of[3], (D,), ((0, 8),), -0.2, 0.2)), 0.5, 2.0),
        "expert_ids": draw_expert_ids(jax.random.fold_in(streams_of[10], 71), 0),
        "slot_index": draw_slot_index(jax.random.fold_in(streams_of[10], 71), 0),
        "gate_prob": jnp.clip(0.1 + 0.9 * jax.random.uniform(streams_of[6], (TOKENS, 2), jnp.float32) ** levels(streams_of[6], (TOKENS, 2), ((0, 32),), -0.2, 0.2), 0.1, 1.0),
        "w_gate": centred(streams_of[7], (2 * EXPERTS, D, HID // 2), D ** -0.5, 0.0625, ((0, 32), (2, 8))),
        "w_up": centred(streams_of[8], (2 * EXPERTS, D, HID // 2), D ** -0.5, 0.0625, ((0, 32), (2, 8))),
        "w_down": centred(streams_of[9], (2 * EXPERTS, HID // 2, D), HID ** -0.5, 0.09375, ((0, 32), (1, 8))),
    }


epsilon = 1e-05

def reference(attention, out_weight, residual, norm_gain, expert_ids, slot_index, gate_prob, w_gate, w_up, w_down):
    projected = jnp.dot(attention, out_weight, preferred_element_type=jnp.float32)
    hidden_state = residual.astype(jnp.float32) + projected
    mean_square = lax.optimization_barrier(jnp.mean(hidden_state * hidden_state, axis=1, keepdims=True))
    normed = (hidden_state * lax.rsqrt(mean_square + epsilon) * norm_gain).astype(jnp.bfloat16)
    blocks = TOKENS // TOK_DEV
    target = jnp.where(slot_index >= 0, expert_ids * CAP + slot_index, -1).reshape(blocks, TOK_DEV, 2)
    token_blocks = normed.reshape(blocks, TOK_DEV, D)
    positions = jnp.arange(EXPERTS * CAP, dtype=jnp.int32)

    def dispatch(block_item):
        block_target, block_rows = block_item
        chosen = jnp.any(positions[:, None, None] == block_target[None, :, :], axis=2)
        return jnp.dot(chosen.astype(jnp.bfloat16), block_rows, preferred_element_type=jnp.float32).astype(jnp.bfloat16)
    buffers = lax.map(dispatch, (target, token_blocks)).reshape(blocks, EXPERTS, CAP, D)
    part_size = HID // (2 * N_MP)

    def run_expert(expert_index):
        slot_rows = lax.dynamic_index_in_dim(buffers, expert_index, 1, keepdims=False).reshape(blocks * CAP, D)
        running = jnp.zeros((blocks * CAP, D), jnp.float32)
        for half_index in range(2):
            row_of = 2 * expert_index + half_index
            gate_val = jnp.dot(slot_rows, lax.dynamic_index_in_dim(w_gate, row_of, 0, False), preferred_element_type=jnp.float32)
            up_val = jnp.dot(slot_rows, lax.dynamic_index_in_dim(w_up, row_of, 0, False), preferred_element_type=jnp.float32)
            active = (jax.nn.silu(gate_val) * up_val).astype(jnp.bfloat16)
            down_rows = lax.dynamic_index_in_dim(w_down, row_of, 0, False).reshape(N_MP, part_size, D).astype(jnp.float32)
            products = jnp.einsum('smp,mpd->msd', active.reshape(blocks * CAP, N_MP, part_size).astype(jnp.float32), down_rows)
            rounded = lax.optimization_barrier(products.astype(jnp.bfloat16)).astype(jnp.float32)
            half_sum = lax.optimization_barrier(lax.optimization_barrier(jnp.sum(rounded, axis=0)).astype(jnp.bfloat16))
            running = running + half_sum.astype(jnp.float32)
        whole = lax.optimization_barrier(running.astype(jnp.bfloat16)).astype(jnp.float32)
        return whole.reshape(blocks, CAP, D)
    expert_out = lax.map(run_expert, jnp.arange(EXPERTS, dtype=jnp.int32))
    block_ids = expert_ids.reshape(blocks, TOK_DEV, 2)
    block_slots = slot_index.reshape(blocks, TOK_DEV, 2)
    block_index = jnp.broadcast_to(jnp.arange(blocks, dtype=jnp.int32)[:, None, None], (blocks, TOK_DEV, 2))
    picked = expert_out[block_ids, block_index, jnp.maximum(block_slots, 0)]
    weight = jnp.where(block_slots >= 0, gate_prob.reshape(blocks, TOK_DEV, 2), jnp.zeros((), jnp.float32))
    expert_mix = lax.optimization_barrier(jnp.sum(picked * weight[..., None], axis=2)).reshape(TOKENS, D)
    return (hidden_state + expert_mix).astype(jnp.bfloat16)
```

```python
import jax
import jax.numpy as jnp
from jax import lax
from jax.experimental import pallas as pl
from jax.experimental.pallas import tpu as pltpu
from jax.sharding import Mesh
from jax.sharding import PartitionSpec as P

epsilon = 1e-05

EXPERT = ("z_lo", "y", "x")
MP = ("z_hi", "core")
SIZES = (2, 4, 4, 4, 2)
NX = 4
NY = 4
NZ = 4
N_MP = 8

TOK = 128
D = 7168
SHARD = D // N_MP
FEAT = 448
W_ROWS = 112
GROUPS = 32
HID = 256
SHARE = 10
UNITS = 5
QUARTER = D // NZ
ROWS = GROUPS * 8
PAIRS = GROUPS * 2
GAIN_ROWS = 16
MLP_ROWS = ROWS + PAIRS
HEAD = 512
TAIL = SHARD - HEAD

BF16 = jnp.bfloat16
F32 = jnp.float32
VMEM_LIMIT = 50 * 1024 * 1024


def dot(a, b, dims=((1,), (0,))):
    return lax.dot_general(a, b, (dims, ((), ())), preferred_element_type=F32)


def iota(shape, dim):
    return lax.broadcasted_iota(jnp.int32, shape, dim)


def shift(value, axis, size, step):
    if step == 0:
        return value
    return lax.ppermute(value, axis, [(i, (i + step) % size) for i in range(size)])


def swap(value, axis):
    return lax.ppermute(value, axis, [(0, 1), (1, 0)])


def shard_of(place, step, other):
    z = lax.rem(place[0] - step + NZ, NZ)
    core = 1 - place[1] if other else place[1]
    return 2 * z + core


def call(kernel, out_shape, flops, moved, **kwargs):
    return pl.pallas_call(
        kernel,
        out_shape=out_shape,
        compiler_params=pltpu.CompilerParams(vmem_limit_bytes=VMEM_LIMIT),
        cost_estimate=pl.CostEstimate(flops=flops, bytes_accessed=moved, transcendentals=0),
        **kwargs,
    )


SMEM = pl.BlockSpec(memory_space=pltpu.SMEM)
VMEM = pl.BlockSpec(memory_space=pltpu.VMEM)
ANY = pl.BlockSpec(memory_space=pl.ANY)


def whole(shape):
    return pl.BlockSpec(shape, lambda step: (0,) * len(shape))


def project_kernel(place, *refs):
    features, blocks, out = refs[:8], refs[8:16], refs[16]
    rows, weights = refs[17:]
    for other in range(2):
        for step in range(NZ):
            rows[shard_of(place, step, other)] = features[other * NZ + step][...]
    for far in range(2):
        for step in range(NX):
            z_lo = lax.rem(place[2] + far, 2)
            x = lax.rem(place[3] - step + NX, NX)
            weights[z_lo * NX + x] = blocks[far * NX + step][...]
    near = weights[0:NX].reshape(FEAT, SHARD)
    later = weights[NX:].reshape(FEAT, SHARD)
    for y in range(NY):
        total = dot(rows[y], near, ((0,), (0,))) + dot(rows[NY + y], later, ((0,), (0,)))
        out[y] = total.astype(BF16)


def project(place, attention, out_weight, residual):
    flipped = attention.T
    features = []
    for step in range(NZ):
        pairs = []
        for y in range(NY):
            for m in range(N_MP):
                z, core = divmod(m // NY * NY + y, 2)
                pairs.append((y * N_MP + m, m % NY * N_MP + (z + step) % NZ * 2 + core))
        features.append(lax.ppermute(flipped, ("y",) + MP, pairs))
    features += [swap(value, "core") for value in features]
    blocks = [shift(out_weight, "x", NX, step) for step in range(NX)]
    far = swap(out_weight, "z_lo")
    blocks += [shift(far, "x", NX, step) for step in range(NX)]
    partial = call(
        project_kernel,
        jax.ShapeDtypeStruct((NY, TOK, SHARD), BF16),
        2 * NY * TOK * 2 * FEAT * SHARD,
        4_000_000,
        in_specs=[SMEM] + [VMEM] * 16,
        out_specs=VMEM,
        scratch_shapes=[
            pltpu.VMEM((N_MP, FEAT, TOK), BF16),
            pltpu.VMEM((2 * NX, W_ROWS, SHARD), BF16),
        ],
    )(place, *features, *blocks)
    terms = lax.all_to_all(partial, "y", split_axis=0, concat_axis=0, tiled=True)
    return residual.astype(F32) + jnp.sum(terms.astype(F32), axis=0)


def dispatch_kernel(place, codes, given, *refs):
    parts, out, scales, normed = refs[:8], refs[8], refs[9], refs[10]
    width = out.shape[3] // 2
    unit = pl.program_id(0)

    @pl.when(unit == 0)
    def _():
        if given is None:
            total = jnp.zeros((1, TOK), F32)
            for part in parts:
                line = part[TOK : TOK + GAIN_ROWS, :].astype(F32)[3:4]
                total = total + line[:, :TOK] + line[:, TOK : 2 * TOK] + line[:, 2 * TOK :]
            scale = jnp.broadcast_to(lax.rsqrt(total / D + epsilon), (TOK, TOK)).T
            scales[...] = scale
        else:
            scale = given[...]
        scale = scale[:, 0:1]
        for other in range(2):
            for step in range(NZ):
                part = parts[other * NZ + step]
                lines = part[TOK : TOK + GAIN_ROWS, :].astype(F32)
                gain = lines[0:1] + lines[1:2] + lines[2:3]
                value = part[0:TOK, :].astype(F32) * scale * gain
                normed[shard_of(place, step, other)] = value.astype(BF16)

    row = iota((ROWS, TOK), 0)
    expert = lax.shift_right_logical(row, 4) * 16

    def hits(code):
        return (code == codes[0:1, :]) | (code == codes[1:2, :])

    @pl.when(unit < NZ)
    def _():
        assign = hits(expert + (row & 7)).astype(F32).astype(BF16)
        for half in range(2):
            value = dot(assign, normed[2 * unit + half]).astype(BF16)
            out[:, 0, :, half * width : (half + 1) * width] = value.reshape(GROUPS, 8, width)

    @pl.when(unit == NZ)
    def _():
        hit = hits(expert + 8 + (row & 1))
        quarter = lax.shift_right_logical(row & 7, 1)
        for half in range(2):
            value = jnp.zeros((ROWS, width), F32)
            for q in range(NZ):
                assign = (hit & (quarter == q)).astype(F32).astype(BF16)
                value = value + dot(assign, normed[2 * q + half])
            value = value.astype(BF16)
            out[:, 0, :, half * width : (half + 1) * width] = value.reshape(GROUPS, 8, width)


def early_dispatch_kernel(place, codes, *refs):
    dispatch_kernel(place, codes, None, *refs)


def late_dispatch_kernel(place, codes, given, *refs):
    dispatch_kernel(place, codes, given, *refs[:9], None, refs[9])


def parts_of(mine):
    parts = [shift(mine, "z_hi", NZ, step) for step in range(NZ)]
    return parts + [swap(value, "core") for value in parts]


def slab_of(width):
    return jax.ShapeDtypeStruct((GROUPS, UNITS, 8, 2 * width), BF16)


def dispatch(place, codes, parts, width, scales):
    out = pl.BlockSpec((GROUPS, 1, 8, 2 * width), lambda step: (0, step, 0, 0))
    shape = jax.ShapeDtypeStruct((TOK, TOK), F32)
    early = scales is None
    return call(
        early_dispatch_kernel if early else late_dispatch_kernel,
        (slab_of(width), shape) if early else slab_of(width),
        2 * 2 * ROWS * TOK * N_MP * width,
        ROWS * N_MP * width * 4,
        grid=(UNITS,),
        in_specs=[SMEM, whole((2, TOK))]
        + ([] if early else [whole((TOK, TOK))])
        + [whole((TOK + GAIN_ROWS, width))] * 8,
        out_specs=[out, whole((TOK, TOK))] if early else out,
        scratch_shapes=[pltpu.VMEM((N_MP, TOK, width), BF16)],
    )(place, codes, *([] if early else [scales]), *parts)


def terms_of(value):
    first = lax.reduce_precision(value, 8, 7)
    second = lax.reduce_precision(value - first, 8, 7)
    return [first, second, value - first - second]


def load(sources, buffers, sems, cut):
    copies = []
    for j in range(N_MP):
        copies.append([])
        for index, source in enumerate(sources):
            copy = pltpu.make_async_copy(source.at[cut(j)], buffers.at[index, j], sems.at[index, j])
            copy.start()
            copies[j].append(copy)
    return copies


def rows_cut(begin, width):
    return lambda j: pl.ds(j * SHARD + begin, width)


def columns_cut(begin, width):
    return lambda j: (slice(None), pl.ds(j * SHARD + begin, width))


def accumulate(units, copies, buffers, sums, prior):
    width = units.shape[3]
    for q in range(NZ):
        pair, row = iota((PAIRS, ROWS), 0), iota((PAIRS, ROWS), 1)
        place = lax.shift_right_logical(pair, 1) * 8 + 2 * q + (pair & 1)
        pick = (row == place).astype(F32).astype(BF16)
        head = units[:, q].reshape(ROWS, width)
        tail = dot(pick, units[:, NZ].reshape(ROWS, width)).astype(BF16)
        value = jnp.concatenate([head, tail], axis=0)
        for copy in copies[2 * q] + copies[2 * q + 1]:
            copy.wait()
        for index in range(4):
            product = dot(value, buffers[index, 2 * q : 2 * q + 2].reshape(width, HID))
            if q == 0 and prior is None:
                sums[index] = product
            else:
                sums[index] = product + (prior if q == 0 else sums)[index]


def expand(active, copies, buffers, out):
    width = buffers.shape[3]
    last = [jnp.zeros((ROWS, width), F32)] * 2
    for q in range(NZ):
        row, pair = iota((ROWS, PAIRS), 0), iota((ROWS, PAIRS), 1)
        place = lax.shift_right_logical(pair, 1) * 8 + 2 * q + (pair & 1)
        spread = (row == place).astype(F32).astype(BF16)
        for half in range(2):
            j = 2 * q + half
            for copy in copies[j]:
                copy.wait()
            value = (dot(active[0], buffers[0, j]) + dot(active[1], buffers[1, j])).astype(BF16)
            columns = slice(half * width, (half + 1) * width)
            out[:, q, :, columns] = value[0:ROWS].reshape(GROUPS, 8, width)
            last[half] = last[half] + dot(spread, value[ROWS:])
    for half in range(2):
        columns = slice(half * width, (half + 1) * width)
        out[:, NZ, :, columns] = last[half].astype(BF16).reshape(GROUPS, 8, width)


def gate_kernel(units, gate_a, up_a, gate_b, up_b, sums, buffers, sems):
    width = buffers.shape[2]
    copies = load((gate_a, up_a, gate_b, up_b), buffers, sems, rows_cut(SHARD - width, width))
    accumulate(units, copies, buffers, sums, None)


def middle_kernel(
    units, prior, gate_a, up_a, gate_b, up_b, down_a, down_b, out, active, gates, downs, sums, gate_sems, down_sems
):
    width = gates.shape[2]
    copies = load((gate_a, up_a, gate_b, up_b), gates, gate_sems, rows_cut(0, width))
    later = load((down_a, down_b), downs, down_sems, columns_cut(0, width))
    accumulate(units, copies, gates, sums, prior)
    for index in range(2):
        active[index] = (jax.nn.silu(sums[2 * index]) * sums[2 * index + 1]).astype(BF16)
    expand(active, later, downs, out)


def down_kernel(active, down_a, down_b, out, downs, sems):
    width = downs.shape[3]
    copies = load((down_a, down_b), downs, sems, columns_cut(SHARD - width, width))
    expand(active, copies, downs, out)


def gate_experts(units, gate, up):
    return call(
        gate_kernel,
        jax.ShapeDtypeStruct((4, MLP_ROWS, HID), F32),
        2 * MLP_ROWS * N_MP * TAIL * HID * 4,
        10_000_000,
        in_specs=[VMEM] + [ANY] * 4,
        out_specs=VMEM,
        scratch_shapes=[pltpu.VMEM((4, N_MP, TAIL, HID), BF16), pltpu.SemaphoreType.DMA((4, N_MP))],
    )(units, gate[0], up[0], gate[1], up[1])


def middle_experts(units, prior, gate, up, down):
    return call(
        middle_kernel,
        (slab_of(HEAD), jax.ShapeDtypeStruct((2, MLP_ROWS, HID), BF16)),
        2 * MLP_ROWS * N_MP * HEAD * HID * 6,
        20_000_000,
        in_specs=[VMEM] * 2 + [ANY] * 6,
        out_specs=[VMEM] * 2,
        scratch_shapes=[
            pltpu.VMEM((4, N_MP, HEAD, HID), BF16),
            pltpu.VMEM((2, N_MP, HID, HEAD), BF16),
            pltpu.VMEM((4, MLP_ROWS, HID), F32),
            pltpu.SemaphoreType.DMA((4, N_MP)),
            pltpu.SemaphoreType.DMA((2, N_MP)),
        ],
    )(units, prior, gate[0], up[0], gate[1], up[1], down[0], down[1])


def down_experts(active, down):
    return call(
        down_kernel,
        slab_of(TAIL),
        2 * MLP_ROWS * N_MP * TAIL * HID * 2,
        6_000_000,
        in_specs=[VMEM] + [ANY] * 2,
        out_specs=VMEM,
        scratch_shapes=[pltpu.VMEM((2, N_MP, HID, TAIL), BF16), pltpu.SemaphoreType.DMA((2, N_MP))],
    )(active, down[0], down[1])


def combine_kernel(place, codes, probs, head, tail, keep, give):
    step = pl.program_id(0)
    width = keep.shape[2]
    column = iota((TOK, ROWS), 1)
    expert = lax.shift_right_logical(column, 4) * 16

    def mixing(code, mask):
        mixed = jnp.zeros((TOK, ROWS), F32)
        for choice in range(2):
            hit = code == codes[:, choice : choice + 1]
            hit = hit if mask is None else hit & mask
            mixed = mixed + jnp.where(hit, probs[:, choice : choice + 1], 0.0)
        upper = mixed.astype(BF16)
        return upper, (mixed - upper.astype(F32)).astype(BF16)

    quarter = lax.shift_right_logical(column & 7, 1) == step
    value = jnp.zeros((TOK, 2 * width), F32)
    for mix, slab in (
        (mixing(expert + (column & 7), None), head),
        (mixing(expert + 8 + (column & 1), quarter), tail),
    ):
        slots = slab[:, 0].reshape(ROWS, 2 * width)
        value = value + dot(mix[0], slots) + dot(mix[1], slots)
    value = value.astype(BF16)

    @pl.when(place[1] == 0)
    def _():
        keep[0], give[0] = value[:, :width], value[:, width:]

    @pl.when(place[1] == 1)
    def _():
        keep[0], give[0] = value[:, width:], value[:, :width]


def combine(place, codes, probs, returned):
    width = returned.shape[3] // 2
    slab = (GROUPS, 1, 8, 2 * width)
    shape = jax.ShapeDtypeStruct((NZ, TOK, width), BF16)
    keep, give = call(
        combine_kernel,
        (shape, shape),
        2 * 4 * TOK * ROWS * N_MP * width,
        ROWS * N_MP * width * 4,
        grid=(NZ,),
        in_specs=[
            SMEM,
            whole((TOK, 2)),
            whole((TOK, 2)),
            pl.BlockSpec(slab, lambda step: (0, step, 0, 0)),
            pl.BlockSpec(slab, lambda step: (0, NZ, 0, 0)),
        ],
        out_specs=[pl.BlockSpec((1, TOK, width), lambda step: (step, 0, 0))] * 2,
    )(place, codes, probs, returned, returned)
    both = (keep.astype(F32) + swap(give, "core").astype(F32)).astype(BF16)
    total = lax.dynamic_index_in_dim(both, place[0], 0, False).astype(F32)
    for step in range(1, NZ):
        piece = lax.dynamic_index_in_dim(both, lax.rem(place[0] + step, NZ), 0, False)
        total = total + shift(piece, "z_hi", NZ, step).astype(F32)
    return total


def shards(
    attention,
    out_weight,
    residual,
    norm_gain,
    expert_ids,
    slot_index,
    gate_prob,
    w_gate,
    w_up,
    w_down,
):
    place = jnp.stack([lax.axis_index(name) for name in ("z_hi", "core", "z_lo", "x")])
    place = place.astype(jnp.int32)
    slot = slot_index - SHARE * place[1]
    codes = jnp.where((slot_index >= 0) & (slot >= 0) & (slot < SHARE), 16 * expert_ids + slot, -1)

    hidden_state = project(place, attention, out_weight, residual)
    flat = codes.T
    gains = terms_of(norm_gain)
    squares = jnp.concatenate(terms_of(jnp.sum(hidden_state * hidden_state, axis=1)))
    zeros = jnp.zeros((GAIN_ROWS, SHARD), F32)
    lines = zeros.at[0:3].set(jnp.stack(gains)).at[3, HEAD:].set(squares)
    rows = jnp.concatenate([hidden_state, lines], axis=0).astype(BF16)

    tail, scales = dispatch(place, flat, parts_of(rows[:, HEAD:]), TAIL, None)
    tail, later, gate, up, down = lax.optimization_barrier(
        (tail, rows[:, :HEAD], w_gate[0], w_up[0], w_down[0])
    )
    gate, up, down = [(value, swap(value, "core")) for value in (gate, up, down)]
    exchange = lambda value: lax.all_to_all(value, EXPERT, split_axis=0, concat_axis=0, tiled=True)
    sums = gate_experts(exchange(tail), gate, up)
    head = dispatch(place, flat, parts_of(later), HEAD, scales)
    out_head, active = middle_experts(exchange(head), sums, gate, up, down)
    back = exchange(out_head)
    mix_head = combine(place, codes, gate_prob, back)
    mix_tail = combine(place, codes, gate_prob, exchange(down_experts(active, down)))
    expert_mix = jnp.concatenate([mix_head, mix_tail], axis=1)
    return (hidden_state + expert_mix).astype(BF16)


def solution(mesh):
    fine = Mesh(mesh.devices.reshape(SIZES), EXPERT + MP)
    return jax.shard_map(
        shards,
        mesh=fine,
        in_specs=(
            P(EXPERT, MP),
            P(EXPERT, MP),
            P(EXPERT, MP),
            P(MP),
            P(EXPERT, None),
            P(EXPERT, None),
            P(EXPERT, None),
            P(EXPERT, None, MP),
            P(EXPERT, None, MP),
            P(EXPERT, MP, None),
        ),
        out_specs=P(EXPERT, MP),
        check_vma=False,
    )
```

```python
import jax
import jax.numpy as jnp
import numpy as np
from jax import lax
from jax.experimental import pallas as pl
from jax.experimental.pallas import tpu as pltpu
from jax.sharding import Mesh
from jax.sharding import PartitionSpec as P

epsilon = 1e-05

EXPERT = ("z_lo", "y", "x")
MP = ("z_hi", "core")
SIZES = (2, 4, 4, 4, 2)
NX = 4
NY = 4
NZ = 4
N_MP = 8

TOK = 128
D = 7168
SHARD = D // N_MP
FEAT = 448
W_ROWS = 112
GROUPS = 32
HID = 256
SHARE = 10
CHUNK = 5
UNITS = 5
QUARTER = D // NZ
ROWS = GROUPS * 8
FOUR = GROUPS * 4
SLOTS = GROUPS * CHUNK
GAIN_ROWS = 16

BF16 = jnp.bfloat16
F32 = jnp.float32
MIB = 1024 * 1024


def dot(a, b, dims=((1,), (0,))):
    return lax.dot_general(a, b, (dims, ((), ())), preferred_element_type=F32)


def iota(shape, dim):
    return lax.broadcasted_iota(jnp.int32, shape, dim)


def shift(value, axis, size, step):
    if step == 0:
        return value
    return lax.ppermute(value, axis, [(i, (i + step) % size) for i in range(size)])


def swap(value, axis):
    return lax.ppermute(value, axis, [(0, 1), (1, 0)])


def shard_of(place, step, other):
    z = lax.rem(place[0] - step + NZ, NZ)
    core = 1 - place[1] if other else place[1]
    return 2 * z + core


def call(kernel, out_shape, flops, moved, limit=24, **kwargs):
    return pl.pallas_call(
        kernel,
        out_shape=out_shape,
        compiler_params=pltpu.CompilerParams(vmem_limit_bytes=limit * MIB),
        cost_estimate=pl.CostEstimate(flops=flops, bytes_accessed=moved, transcendentals=0),
        **kwargs,
    )


SMEM = pl.BlockSpec(memory_space=pltpu.SMEM)
VMEM = pl.BlockSpec(memory_space=pltpu.VMEM)
ANY = pl.BlockSpec(memory_space=pl.ANY)


def whole(shape):
    return pl.BlockSpec(shape, lambda step: (0,) * len(shape))


def project_kernel(place, *refs):
    features, blocks, out = refs[:8], refs[8:12], refs[12]
    rows, weights = refs[13:]
    for other in range(2):
        for step in range(NZ):
            rows[shard_of(place, step, other)] = features[other * NZ + step][...]
    for step in range(NX):
        x = lax.rem(place[3] - step + NX, NX)
        weights[place[2] * NX + x] = blocks[step][0:W_ROWS]
        weights[(1 - place[2]) * NX + x] = blocks[step][W_ROWS:]
    near = weights[0:NX].reshape(FEAT, SHARD)
    later = weights[NX:].reshape(FEAT, SHARD)
    for y in range(NY):
        total = dot(rows[y], near, ((0,), (0,))) + dot(rows[NY + y], later, ((0,), (0,)))
        out[y] = total.astype(BF16)


def project(place, attention, out_weight, residual):
    flipped = attention.T
    features = []
    for step in range(NZ):
        pairs = []
        for y in range(NY):
            for m in range(N_MP):
                z, core = divmod(m // NY * NY + y, 2)
                pairs.append((y * N_MP + m, m % NY * N_MP + (z + step) % NZ * 2 + core))
        features.append(lax.ppermute(flipped, ("y",) + MP, pairs))
    features += [swap(value, "core") for value in features]
    both = jnp.concatenate([out_weight, swap(out_weight, "z_lo")], axis=0)
    blocks = [shift(both, "x", NX, step) for step in range(NX)]
    partial = call(
        project_kernel,
        jax.ShapeDtypeStruct((NY, TOK, SHARD), BF16),
        2 * NY * TOK * 2 * FEAT * SHARD,
        4_000_000,
        in_specs=[SMEM] + [VMEM] * 12,
        out_specs=VMEM,
        scratch_shapes=[
            pltpu.VMEM((N_MP, FEAT, TOK), BF16),
            pltpu.VMEM((2 * NX, W_ROWS, SHARD), BF16),
        ],
    )(place, *features, *blocks)
    terms = lax.all_to_all(partial, "y", split_axis=0, concat_axis=0, tiled=True)
    return residual.astype(F32) + jnp.sum(terms.astype(F32), axis=0)


def unit_rows(index, single):
    group = lax.shift_right_logical(index, 3)
    if single:
        return (index & 7) * GROUPS + group
    return (lax.shift_right_logical(index, 2) & 1) * FOUR + group * 4 + (index & 3)


def selection(single, back):
    shape = (ROWS, ROWS)
    hit = iota(shape, int(back)) == unit_rows(iota(shape, 1 - int(back)), single)
    return hit.astype(F32).astype(BF16)


def columns(j):
    return slice(j % 2 * SHARD, (j % 2 + 1) * SHARD)


def by_features(units, rows):
    pick = selection(False, False)
    for unit in range(4):
        value = dot(pick, units[:, unit].reshape(ROWS, SHARD)).astype(BF16)
        for half in range(2):
            j = 4 * half + unit
            rows[j // 2, 0:FOUR, columns(j)] = value[half * FOUR : (half + 1) * FOUR]
    value = dot(selection(True, False), units[:, 4].reshape(ROWS, SHARD)).astype(BF16)
    for j in range(N_MP):
        rows[j // 2, FOUR:, columns(j)] = value[j * GROUPS : (j + 1) * GROUPS]


def by_units(rows, out):
    pick = selection(False, True)
    for unit in range(4):
        halves = [rows[j // 2, 0:FOUR, columns(j)] for j in (unit, 4 + unit)]
        value = dot(pick, jnp.concatenate(halves, axis=0)).astype(BF16)
        out[:, unit] = value.reshape(GROUPS, 8, SHARD)
    eighths = [rows[j // 2, FOUR:, columns(j)] for j in range(N_MP)]
    value = dot(selection(True, True), jnp.concatenate(eighths, axis=0)).astype(BF16)
    out[:, 4] = value.reshape(GROUPS, 8, SHARD)


def slot_codes(chunk):
    group, slot = np.divmod(np.arange(FOUR), 4)
    four = group // 2 * 16 + chunk * CHUNK + slot
    fifth = np.arange(GROUPS) // 2 * 16 + chunk * CHUNK + 4
    return np.concatenate([four, fifth]).astype(np.int32)


def send_rows(codes, slots, normed, out, rows):
    hit = (slots[...] == codes[0:1, :]) | (slots[...] == codes[1:2, :])
    assign = hit.astype(F32).astype(BF16)
    for j in range(N_MP):
        rows[j // 2, :, columns(j)] = dot(assign, normed[j]).astype(BF16)
    by_units(rows, out)


def first_kernel(place, codes, slots, *refs):
    parts, normed, out, rows = refs[:8], refs[8], refs[9], refs[10]
    total = jnp.zeros((TOK, 1), F32)
    for part in parts:
        value = part[0:TOK, :].astype(F32)
        total = total + jnp.sum(value * value, axis=1, keepdims=True)
    scale = lax.rsqrt(total / D + epsilon)
    for other in range(2):
        for step in range(NZ):
            part = parts[other * NZ + step]
            lines = part[TOK : TOK + GAIN_ROWS, :].astype(F32)
            gain = lines[0:1] + lines[1:2] + lines[2:3]
            value = part[0:TOK, :].astype(F32) * scale * gain
            normed[shard_of(place, step, other)] = value.astype(BF16)
    send_rows(codes, slots, normed, out, rows)


def second_kernel(codes, slots, normed, out, rows):
    send_rows(codes, slots, normed, out, rows)


SLAB = (GROUPS, UNITS, 8, SHARD)
SLAB_SHAPE = jax.ShapeDtypeStruct(SLAB, BF16)
ROW_SCRATCH = pltpu.VMEM((NZ, SLOTS, QUARTER), BF16)


def dispatch(place, codes, hidden_state, norm_gain):
    lines = jnp.zeros((GAIN_ROWS, SHARD), F32).at[0:3].set(jnp.stack(terms_of(norm_gain)))
    mine = jnp.concatenate([hidden_state, lines], axis=0).astype(BF16)
    parts = [shift(mine, "z_hi", NZ, step) for step in range(NZ)]
    parts += [swap(value, "core") for value in parts]
    slots = [jnp.asarray(slot_codes(chunk)).reshape(SLOTS, 1) for chunk in range(2)]
    normed, one = call(
        first_kernel,
        (jax.ShapeDtypeStruct((N_MP, TOK, SHARD), BF16), SLAB_SHAPE),
        2_000_000_000,
        6_000_000,
        in_specs=[SMEM] + [VMEM] * 10,
        out_specs=[VMEM, VMEM],
        scratch_shapes=[ROW_SCRATCH],
    )(place, codes, slots[0], *parts)
    two = call(
        second_kernel,
        SLAB_SHAPE,
        1_000_000_000,
        4_000_000,
        in_specs=[VMEM] * 3,
        out_specs=VMEM,
        scratch_shapes=[ROW_SCRATCH],
    )(codes, slots[1], normed)
    return one, two


def terms_of(value):
    first = lax.reduce_precision(value, 8, 7)
    second = lax.reduce_precision(value - first, 8, 7)
    return [first, second, value - first - second]


def load(sources, buffers, sems, cut):
    copies = []
    for q in range(NZ):
        copies.append([])
        for index, source in enumerate(sources):
            copy = pltpu.make_async_copy(source.at[cut(q)], buffers.at[index, q], sems.at[index, q])
            copy.start()
            copies[q].append(copy)
    return copies


def rows_cut(q):
    return pl.ds(q * QUARTER, QUARTER)


def columns_cut(q):
    return slice(None), pl.ds(q * QUARTER, QUARTER)


def experts_kernel(
    units, gate_a, up_a, gate_b, up_b, down_a, down_b, out, rows, gates, downs, sums, active, gate_sems, down_sems
):
    first = load((gate_a, up_a, gate_b, up_b), gates, gate_sems, rows_cut)
    second = load((down_a, down_b), downs, down_sems, columns_cut)
    by_features(units, rows)
    for q in range(NZ):
        for copy in first[q]:
            copy.wait()
        for index in range(4):
            product = dot(rows[q], gates[index, q])
            sums[index] = product if q == 0 else sums[index] + product
    for index in range(2):
        active[index] = (jax.nn.silu(sums[2 * index]) * sums[2 * index + 1]).astype(BF16)
    for q in range(NZ):
        for copy in second[q]:
            copy.wait()
        rows[q] = (dot(active[0], downs[0, q]) + dot(active[1], downs[1, q])).astype(BF16)
    by_units(rows, out)


def experts(arrived, gate, up, down):
    return call(
        experts_kernel,
        SLAB_SHAPE,
        2 * SLOTS * D * HID * 6,
        27_000_000,
        60,
        in_specs=[VMEM] + [ANY] * 6,
        out_specs=VMEM,
        scratch_shapes=[
            ROW_SCRATCH,
            pltpu.VMEM((4, NZ, QUARTER, HID), BF16),
            pltpu.VMEM((2, NZ, HID, QUARTER), BF16),
            pltpu.VMEM((4, SLOTS, HID), F32),
            pltpu.VMEM((2, SLOTS, HID), BF16),
            pltpu.SemaphoreType.DMA((4, NZ)),
            pltpu.SemaphoreType.DMA((2, NZ)),
        ],
    )(arrived, gate[0], up[0], gate[1], up[1], down[0], down[1])


def mix(step, codes, probs, slots, units, rows, weights):
    @pl.when(step == 0)
    def _():
        by_features(units, rows)
        mixed = jnp.zeros((TOK, SLOTS), F32)
        for choice in range(2):
            hit = slots[...] == codes[:, choice : choice + 1]
            mixed = mixed + jnp.where(hit, probs[:, choice : choice + 1], 0.0)
        upper = mixed.astype(BF16)
        weights[0] = upper
        weights[1] = (mixed - upper.astype(F32)).astype(BF16)

    value = rows[step]
    return dot(weights[0], value) + dot(weights[1], value)


def early_kernel(codes, probs, slots, units, out, rows, weights):
    out[0] = mix(pl.program_id(0), codes, probs, slots, units, rows, weights)


def late_kernel(place, codes, probs, slots, units, prior, keep, give, rows, weights):
    value = mix(pl.program_id(0), codes, probs, slots, units, rows, weights)
    value = (prior[0] + value).astype(BF16)

    @pl.when(place[1] == 0)
    def _():
        keep[0], give[0] = value[:, :SHARD], value[:, SHARD:]

    @pl.when(place[1] == 1)
    def _():
        keep[0], give[0] = value[:, SHARD:], value[:, :SHARD]


def combine(place, codes, probs, returned):
    slots = [jnp.asarray(slot_codes(chunk)).reshape(1, SLOTS) for chunk in range(2)]
    common = [whole((TOK, 2)), whole((TOK, 2)), whole((1, SLOTS)), whole(SLAB)]
    pair = pl.BlockSpec((1, TOK, QUARTER), lambda step: (step, 0, 0))
    scratch = [ROW_SCRATCH, pltpu.VMEM((2, TOK, SLOTS), BF16)]
    prior = call(
        early_kernel,
        jax.ShapeDtypeStruct((NZ, TOK, QUARTER), F32),
        2_500_000_000,
        6_000_000,
        grid=(NZ,),
        in_specs=common,
        out_specs=pair,
        scratch_shapes=scratch,
    )(codes, probs, slots[0], returned[0])
    shape = jax.ShapeDtypeStruct((NZ, TOK, SHARD), BF16)
    keep, give = call(
        late_kernel,
        (shape, shape),
        2_500_000_000,
        7_000_000,
        grid=(NZ,),
        in_specs=[SMEM] + common + [pair],
        out_specs=[pl.BlockSpec((1, TOK, SHARD), lambda step: (step, 0, 0))] * 2,
        scratch_shapes=scratch,
    )(place, codes, probs, slots[1], returned[1], prior)
    both = (keep.astype(F32) + swap(give, "core").astype(F32)).astype(BF16)
    total = lax.dynamic_index_in_dim(both, place[0], 0, False).astype(F32)
    for step in range(1, NZ):
        piece = lax.dynamic_index_in_dim(both, lax.rem(place[0] + step, NZ), 0, False)
        total = total + shift(piece, "z_hi", NZ, step).astype(F32)
    return total


def shards(
    attention,
    out_weight,
    residual,
    norm_gain,
    expert_ids,
    slot_index,
    gate_prob,
    w_gate,
    w_up,
    w_down,
):
    place = jnp.stack([lax.axis_index(name) for name in ("z_hi", "core", "z_lo", "x")])
    place = place.astype(jnp.int32)
    slot = slot_index - SHARE * place[1]
    codes = jnp.where((slot_index >= 0) & (slot >= 0) & (slot < SHARE), 16 * expert_ids + slot, -1)

    hidden_state = project(place, attention, out_weight, residual)
    one, two = dispatch(place, codes.T, hidden_state, norm_gain)
    one, gate, up, down = lax.optimization_barrier((one, w_gate[0], w_up[0], w_down[0]))
    gate, up, down = [(value, swap(value, "core")) for value in (gate, up, down)]
    two, gate, up, down = lax.optimization_barrier((two, gate, up, down))
    returned = []
    for rows in (one, two):
        arrived = lax.all_to_all(rows, EXPERT, split_axis=0, concat_axis=0, tiled=True)
        half_out = experts(arrived, gate, up, down)
        returned.append(lax.all_to_all(half_out, EXPERT, split_axis=0, concat_axis=0, tiled=True))
    expert_mix = combine(place, codes, gate_prob, returned)
    return (hidden_state + expert_mix).astype(BF16)


def solution(mesh):
    fine = Mesh(mesh.devices.reshape(SIZES), EXPERT + MP)
    return jax.shard_map(
        shards,
        mesh=fine,
        in_specs=(
            P(EXPERT, MP),
            P(EXPERT, MP),
            P(EXPERT, MP),
            P(MP),
            P(EXPERT, None),
            P(EXPERT, None),
            P(EXPERT, None),
            P(EXPERT, None, MP),
            P(EXPERT, None, MP),
            P(EXPERT, MP, None),
        ),
        out_specs=P(EXPERT, MP),
        check_vma=False,
    )
```

```python
import jax
import jax.numpy as jnp
from jax import lax
from jax.experimental import pallas as pl
from jax.experimental.pallas import tpu as pltpu
from jax.sharding import Mesh
from jax.sharding import PartitionSpec as P

epsilon = 1e-05

EXPERT = ("z_lo", "y", "x")
MP = ("z_hi", "core")
SIZES = (2, 4, 4, 4, 2)
NX = 4
NY = 4
NZ = 4
N_MP = 8

TOK = 128
D = 7168
SHARD = D // N_MP
FEAT = 448
W_ROWS = 112
GROUPS = 32
HID = 256
SHARE = 10
CHUNK = 5
UNITS = 5
QUARTER = D // NZ
ROWS = GROUPS * 8
FOUR = GROUPS * 4
SLOTS = GROUPS * CHUNK
GAIN_ROWS = 16

BF16 = jnp.bfloat16
F32 = jnp.float32
MIB = 1024 * 1024


def dot(a, b, dims=((1,), (0,))):
    return lax.dot_general(a, b, (dims, ((), ())), preferred_element_type=F32)


def iota(shape, dim):
    return lax.broadcasted_iota(jnp.int32, shape, dim)


def shift(value, axis, size, step):
    if step == 0:
        return value
    return lax.ppermute(value, axis, [(i, (i + step) % size) for i in range(size)])


def swap(value, axis):
    return lax.ppermute(value, axis, [(0, 1), (1, 0)])


def shard_of(place, step, other):
    z = lax.rem(place[0] - step + NZ, NZ)
    core = 1 - place[1] if other else place[1]
    return 2 * z + core


def call(kernel, out_shape, flops, moved, limit=24, **kwargs):
    return pl.pallas_call(
        kernel,
        out_shape=out_shape,
        compiler_params=pltpu.CompilerParams(vmem_limit_bytes=limit * MIB),
        cost_estimate=pl.CostEstimate(flops=flops, bytes_accessed=moved, transcendentals=0),
        **kwargs,
    )


SMEM = pl.BlockSpec(memory_space=pltpu.SMEM)
HBM = pl.BlockSpec(memory_space=pltpu.HBM)


def whole(shape):
    return pl.BlockSpec(shape, lambda step: (0,) * len(shape))


def project_kernel(place, *refs):
    features, blocks, outs = refs[:8], refs[8:12], refs[12:16]
    rows, weights = refs[16:]
    for other in range(2):
        for step in range(NZ):
            rows[shard_of(place, step, other)] = features[other * NZ + step][...]
    for step in range(NX):
        x = lax.rem(place[3] - step + NX, NX)
        weights[place[2] * NX + x] = blocks[step][0:W_ROWS]
        weights[(1 - place[2]) * NX + x] = blocks[step][W_ROWS:]
    near = weights[0:NX].reshape(FEAT, SHARD)
    later = weights[NX:].reshape(FEAT, SHARD)
    for step, out in enumerate(outs):
        y = lax.rem(place[4] + step, NY)
        total = dot(rows[y], near, ((0,), (0,))) + dot(rows[NY + y], later, ((0,), (0,)))
        out[...] = total.astype(out.dtype)


def project(place, attention, out_weight, residual):
    flipped = attention.T
    features = []
    for step in range(NZ):
        pairs = []
        for y in range(NY):
            for m in range(N_MP):
                z, core = divmod(m // NY * NY + y, 2)
                pairs.append((y * N_MP + m, m % NY * N_MP + (z + step) % NZ * 2 + core))
        features.append(lax.ppermute(flipped, ("y",) + MP, pairs))
    features += [swap(value, "core") for value in features]
    both = jnp.concatenate([out_weight, swap(out_weight, "z_lo")], axis=0)
    blocks = [shift(both, "x", NX, step) for step in range(NX)]
    partial = call(
        project_kernel,
        [jax.ShapeDtypeStruct((TOK, SHARD), BF16 if step else F32) for step in range(NY)],
        2 * NY * TOK * 2 * FEAT * SHARD,
        4_000_000,
        16,
        grid=(1,),
        in_specs=[SMEM] + [whole((FEAT, TOK))] * 8 + [whole((2 * W_ROWS, SHARD))] * 4,
        out_specs=[whole((TOK, SHARD))] * NY,
        scratch_shapes=[
            pltpu.VMEM((N_MP, FEAT, TOK), BF16),
            pltpu.VMEM((2 * NX, W_ROWS, SHARD), BF16),
        ],
    )(place, *features, *blocks)
    total = residual.astype(F32) + partial[0]
    for step in range(1, NY):
        total = total + shift(partial[step], "y", NY, step).astype(F32)
    return total


def unit_rows(index, single):
    group = lax.shift_right_logical(index, 3)
    if single:
        return (index & 7) * GROUPS + group
    return (lax.shift_right_logical(index, 2) & 1) * FOUR + group * 4 + (index & 3)


def selection(single, back):
    shape = (ROWS, ROWS)
    hit = iota(shape, int(back)) == unit_rows(iota(shape, 1 - int(back)), single)
    return hit.astype(F32).astype(BF16)


def columns(j):
    return slice(j % 2 * SHARD, (j % 2 + 1) * SHARD)


def by_features(units, rows):
    pick = selection(False, False)
    for unit in range(4):
        value = dot(pick, units[:, unit].reshape(ROWS, SHARD)).astype(BF16)
        for half in range(2):
            j = 4 * half + unit
            rows[j // 2, 0:FOUR, columns(j)] = value[half * FOUR : (half + 1) * FOUR]
    value = dot(selection(True, False), units[:, 4].reshape(ROWS, SHARD)).astype(BF16)
    for j in range(N_MP):
        rows[j // 2, FOUR:, columns(j)] = value[j * GROUPS : (j + 1) * GROUPS]


def by_units(rows, out):
    pick = selection(False, True)
    for unit in range(4):
        halves = [rows[j // 2, 0:FOUR, columns(j)] for j in (unit, 4 + unit)]
        value = dot(pick, jnp.concatenate(halves, axis=0)).astype(BF16)
        out[:, unit] = value.reshape(GROUPS, 8, SHARD)
    eighths = [rows[j // 2, FOUR:, columns(j)] for j in range(N_MP)]
    value = dot(selection(True, True), jnp.concatenate(eighths, axis=0)).astype(BF16)
    out[:, 4] = value.reshape(GROUPS, 8, SHARD)


def slot_codes(shape, dim, chunk):
    index = iota(shape, dim)
    four = lax.shift_right_logical(index, 3) * 16 + (index & 3)
    fifth = lax.shift_right_logical(index - FOUR, 1) * 16 + 4
    return jnp.where(index < FOUR, four, fifth) + chunk * CHUNK


def send_rows(codes, chunk, normed, out, rows):
    slots = slot_codes((SLOTS, TOK), 0, chunk)
    hit = (slots == codes[0:1, :]) | (slots == codes[1:2, :])
    assign = hit.astype(F32).astype(BF16)
    for j in range(N_MP):
        rows[j // 2, :, columns(j)] = dot(assign, normed[j]).astype(BF16)
    by_units(rows, out)


def first_kernel(place, codes, *refs):
    parts, normed, out, rows = refs[:8], refs[8], refs[9], refs[10]
    total = jnp.zeros((TOK, 1), F32)
    for part in parts:
        value = part[0:TOK, :].astype(F32)
        total = total + jnp.sum(value * value, axis=1, keepdims=True)
    scale = lax.rsqrt(total / D + epsilon)
    for other in range(2):
        for step in range(NZ):
            part = parts[other * NZ + step]
            lines = part[TOK : TOK + GAIN_ROWS, :].astype(F32)
            gain = lines[0:1] + lines[1:2] + lines[2:3]
            value = part[0:TOK, :].astype(F32) * scale * gain
            normed[shard_of(place, step, other)] = value.astype(BF16)
    send_rows(codes, 0, normed, out, rows)


def second_kernel(codes, normed, out, rows):
    send_rows(codes, 1, normed, out, rows)


SLAB = (GROUPS, UNITS, 8, SHARD)
SLAB_SHAPE = pltpu.HBM(SLAB, BF16)
ROW_SCRATCH = pltpu.VMEM((NZ, SLOTS, QUARTER), BF16)


def dispatch(place, codes, hidden_state, norm_gain):
    lines = jnp.zeros((GAIN_ROWS, SHARD), F32).at[0:3].set(jnp.stack(terms_of(norm_gain)))
    mine = jnp.concatenate([hidden_state, lines], axis=0).astype(BF16)
    parts = [shift(mine, "z_hi", NZ, step) for step in range(NZ)]
    parts += [swap(value, "core") for value in parts]
    normed, one = call(
        first_kernel,
        (pltpu.HBM((N_MP, TOK, SHARD), BF16), SLAB_SHAPE),
        2_000_000_000,
        6_000_000,
        grid=(1,),
        in_specs=[SMEM, whole((2, TOK))] + [whole((TOK + GAIN_ROWS, SHARD))] * 8,
        out_specs=[whole((N_MP, TOK, SHARD)), whole(SLAB)],
        scratch_shapes=[ROW_SCRATCH],
    )(place, codes, *parts)
    two = call(
        second_kernel,
        SLAB_SHAPE,
        1_000_000_000,
        4_000_000,
        grid=(1,),
        in_specs=[whole((2, TOK)), whole((N_MP, TOK, SHARD))],
        out_specs=whole(SLAB),
        scratch_shapes=[ROW_SCRATCH],
    )(codes, normed)
    return one, two


def terms_of(value):
    first = lax.reduce_precision(value, 8, 7)
    second = lax.reduce_precision(value - first, 8, 7)
    return [first, second, value - first - second]


def load(sources, buffers, sems, cut):
    copies = []
    for q in range(NZ):
        copies.append([])
        for index, source in enumerate(sources):
            copy = pltpu.make_async_copy(source.at[cut(q)], buffers.at[index, q], sems.at[index, q])
            copy.start()
            copies[q].append(copy)
    return copies


def rows_cut(q):
    return pl.ds(q * QUARTER, QUARTER)


def columns_cut(q):
    return slice(None), pl.ds(q * QUARTER, QUARTER)


def experts_kernel(
    units, gate_a, up_a, gate_b, up_b, down_a, down_b, out, rows, gates, downs, sums, active, gate_sems, down_sems
):
    first = load((gate_a, up_a, gate_b, up_b), gates, gate_sems, rows_cut)
    second = load((down_a, down_b), downs, down_sems, columns_cut)
    by_features(units, rows)
    for q in range(NZ):
        for copy in first[q]:
            copy.wait()
        for index in range(4):
            product = dot(rows[q], gates[index, q])
            sums[index] = product if q == 0 else sums[index] + product
    for index in range(2):
        active[index] = (jax.nn.silu(sums[2 * index]) * sums[2 * index + 1]).astype(BF16)
    for q in range(NZ):
        for copy in second[q]:
            copy.wait()
        rows[q] = (dot(active[0], downs[0, q]) + dot(active[1], downs[1, q])).astype(BF16)
    by_units(rows, out)


def experts(arrived, gate, up, down):
    return call(
        experts_kernel,
        SLAB_SHAPE,
        2 * SLOTS * D * HID * 6,
        27_000_000,
        34,
        grid=(1,),
        in_specs=[whole(SLAB)] + [HBM] * 6,
        out_specs=whole(SLAB),
        scratch_shapes=[
            ROW_SCRATCH,
            pltpu.VMEM((4, NZ, QUARTER, HID), BF16),
            pltpu.VMEM((2, NZ, HID, QUARTER), BF16),
            pltpu.VMEM((4, SLOTS, HID), F32),
            pltpu.VMEM((2, SLOTS, HID), BF16),
            pltpu.SemaphoreType.DMA((4, NZ)),
            pltpu.SemaphoreType.DMA((2, NZ)),
        ],
    )(arrived, gate[0], up[0], gate[1], up[1], down[0], down[1])


def mix(step, codes, probs, chunk, units, rows, weights):
    @pl.when(step == 0)
    def _():
        by_features(units, rows)
        slots = slot_codes((TOK, SLOTS), 1, chunk)
        mixed = jnp.zeros((TOK, SLOTS), F32)
        for choice in range(2):
            hit = slots == codes[:, choice : choice + 1]
            mixed = mixed + jnp.where(hit, probs[:, choice : choice + 1], 0.0)
        upper = mixed.astype(BF16)
        weights[0] = upper
        weights[1] = (mixed - upper.astype(F32)).astype(BF16)

    value = rows[step]
    return dot(weights[0], value) + dot(weights[1], value)


def early_kernel(codes, probs, units, out, rows, weights):
    out[0] = mix(pl.program_id(0), codes, probs, 0, units, rows, weights)


def late_kernel(place, codes, probs, units, prior, keep, give, rows, weights):
    value = mix(pl.program_id(0), codes, probs, 1, units, rows, weights)
    value = (prior[0] + value).astype(BF16)

    @pl.when(place[1] == 0)
    def _():
        keep[0], give[0] = value[:, :SHARD], value[:, SHARD:]

    @pl.when(place[1] == 1)
    def _():
        keep[0], give[0] = value[:, SHARD:], value[:, :SHARD]


def combine(place, codes, probs, returned):
    common = [whole((TOK, 2)), whole((TOK, 2)), whole(SLAB)]
    pair = pl.BlockSpec((1, TOK, QUARTER), lambda step: (step, 0, 0))
    scratch = [ROW_SCRATCH, pltpu.VMEM((2, TOK, SLOTS), BF16)]
    prior = call(
        early_kernel,
        pltpu.HBM((NZ, TOK, QUARTER), F32),
        2_500_000_000,
        6_000_000,
        grid=(NZ,),
        in_specs=common,
        out_specs=pair,
        scratch_shapes=scratch,
    )(codes, probs, returned[0])
    shape = jax.ShapeDtypeStruct((NZ, TOK, SHARD), BF16)
    keep, give = call(
        late_kernel,
        (shape, shape),
        2_500_000_000,
        7_000_000,
        60,
        grid=(NZ,),
        in_specs=[SMEM] + common + [pair],
        out_specs=[pl.BlockSpec((1, TOK, SHARD), lambda step: (step, 0, 0))] * 2,
        scratch_shapes=scratch,
    )(place, codes, probs, returned[1], prior)
    both = (keep.astype(F32) + swap(give, "core").astype(F32)).astype(BF16)
    total = lax.dynamic_index_in_dim(both, place[0], 0, False).astype(F32)
    for step in range(1, NZ):
        piece = lax.dynamic_index_in_dim(both, lax.rem(place[0] + step, NZ), 0, False)
        total = total + shift(piece, "z_hi", NZ, step).astype(F32)
    return total


def shards(
    attention,
    out_weight,
    residual,
    norm_gain,
    expert_ids,
    slot_index,
    gate_prob,
    w_gate,
    w_up,
    w_down,
):
    place = jnp.stack([lax.axis_index(name) for name in ("z_hi", "core", "z_lo", "x", "y")])
    place = place.astype(jnp.int32)
    slot = slot_index - SHARE * place[1]
    codes = jnp.where((slot_index >= 0) & (slot >= 0) & (slot < SHARE), 16 * expert_ids + slot, -1)

    hidden_state = project(place, attention, out_weight, residual)
    one, two = dispatch(place, codes.T, hidden_state, norm_gain)
    one, gate, up, down = lax.optimization_barrier((one, w_gate[0], w_up[0], w_down[0]))
    gate, up, down = [(value, swap(value, "core")) for value in (gate, up, down)]
    two, gate, up, down = lax.optimization_barrier((two, gate, up, down))
    returned = []
    for rows in (one, two):
        arrived = lax.all_to_all(rows, EXPERT, split_axis=0, concat_axis=0, tiled=True)
        half_out = experts(arrived, gate, up, down)
        returned.append(lax.all_to_all(half_out, EXPERT, split_axis=0, concat_axis=0, tiled=True))
    expert_mix = combine(place, codes, gate_prob, returned)
    return (hidden_state + expert_mix).astype(BF16)


def solution(mesh):
    fine = Mesh(mesh.devices.reshape(SIZES), EXPERT + MP)
    return jax.shard_map(
        shards,
        mesh=fine,
        in_specs=(
            P(EXPERT, MP),
            P(EXPERT, MP),
            P(EXPERT, MP),
            P(MP),
            P(EXPERT, None),
            P(EXPERT, None),
            P(EXPERT, None),
            P(EXPERT, None, MP),
            P(EXPERT, None, MP),
            P(EXPERT, MP, None),
        ),
        out_specs=P(EXPERT, MP),
        check_vma=False,
    )
```

```python
import functools

import jax
import jax.numpy as jnp
from jax import lax
from jax.experimental import pallas as pl
from jax.experimental.pallas import tpu as pltpu
from jax.sharding import Mesh
from jax.sharding import PartitionSpec as P

epsilon = 1e-05

EXPERT = ("z_lo", "y", "x")
MP = ("z_hi", "core")
SIZES = (2, 4, 4, 4, 2)
NX = 4
NY = 4
NZ = 4
N_MP = 8

TOK = 128
D = 7168
SHARD = D // N_MP
FEAT = 448
W_ROWS = 112
GROUPS = 32
HID = 256
SHARE = 10
CHUNK = 5
UNITS = 5
QUARTER = D // NZ
ROWS = GROUPS * 8
FOUR = GROUPS * 4
SLOTS = GROUPS * CHUNK
GAIN_ROWS = 16

BF16 = jnp.bfloat16
F32 = jnp.float32
MIB = 1024 * 1024


def dot(a, b, dims=((1,), (0,))):
    return lax.dot_general(a, b, (dims, ((), ())), preferred_element_type=F32)


def iota(shape, dim):
    return lax.broadcasted_iota(jnp.int32, shape, dim)


def shift(value, axis, size, step):
    if step == 0:
        return value
    return lax.ppermute(value, axis, [(i, (i + step) % size) for i in range(size)])


def swap(value, axis):
    return lax.ppermute(value, axis, [(0, 1), (1, 0)])


def shard_of(place, step, other):
    z = lax.rem(place[0] - step + NZ, NZ)
    core = 1 - place[1] if other else place[1]
    return 2 * z + core


def call(kernel, out_shape, flops, moved, limit=24, **kwargs):
    return pl.pallas_call(
        kernel,
        out_shape=out_shape,
        compiler_params=pltpu.CompilerParams(vmem_limit_bytes=limit * MIB),
        cost_estimate=pl.CostEstimate(flops=flops, bytes_accessed=moved, transcendentals=0),
        **kwargs,
    )


SMEM = pl.BlockSpec(memory_space=pltpu.SMEM)
HBM = pl.BlockSpec(memory_space=pltpu.HBM)


def whole(shape):
    return pl.BlockSpec(shape, lambda step: (0,) * len(shape))


def project_kernel(place, *refs):
    features, blocks, outs = refs[:8], refs[8:12], refs[12:16]
    rows, weights = refs[16:]
    for other in range(2):
        for step in range(NZ):
            rows[shard_of(place, step, other)] = features[other * NZ + step][...]
    for step in range(NX):
        x = lax.rem(place[3] - step + NX, NX)
        weights[place[2] * NX + x] = blocks[step][0:W_ROWS]
        weights[(1 - place[2]) * NX + x] = blocks[step][W_ROWS:]
    near = weights[0:NX].reshape(FEAT, SHARD)
    later = weights[NX:].reshape(FEAT, SHARD)
    for step, out in enumerate(outs):
        y = lax.rem(place[4] + step, NY)
        total = dot(rows[y], near, ((0,), (0,))) + dot(rows[NY + y], later, ((0,), (0,)))
        out[...] = total.astype(out.dtype)


def project(place, attention, out_weight, residual):
    flipped = attention.T
    features = []
    for step in range(NZ):
        pairs = []
        for y in range(NY):
            for m in range(N_MP):
                z, core = divmod(m // NY * NY + y, 2)
                pairs.append((y * N_MP + m, m % NY * N_MP + (z + step) % NZ * 2 + core))
        features.append(lax.ppermute(flipped, ("y",) + MP, pairs))
    features += [swap(value, "core") for value in features]
    both = jnp.concatenate([out_weight, swap(out_weight, "z_lo")], axis=0)
    blocks = [shift(both, "x", NX, step) for step in range(NX)]
    partial = call(
        project_kernel,
        [jax.ShapeDtypeStruct((TOK, SHARD), BF16 if step else F32) for step in range(NY)],
        2 * NY * TOK * 2 * FEAT * SHARD,
        4_000_000,
        16,
        grid=(1,),
        in_specs=[SMEM] + [whole((FEAT, TOK))] * 8 + [whole((2 * W_ROWS, SHARD))] * 4,
        out_specs=[whole((TOK, SHARD))] * NY,
        scratch_shapes=[
            pltpu.VMEM((N_MP, FEAT, TOK), BF16),
            pltpu.VMEM((2 * NX, W_ROWS, SHARD), BF16),
        ],
    )(place, *features, *blocks)
    total = residual.astype(F32) + partial[0]
    for step in range(1, NY):
        total = total + shift(partial[step], "y", NY, step).astype(F32)
    return total


def unit_rows(index, single):
    group = lax.shift_right_logical(index, 3)
    if single:
        return (index & 7) * GROUPS + group
    return (lax.shift_right_logical(index, 2) & 1) * FOUR + group * 4 + (index & 3)


def selection(single, back):
    shape = (ROWS, ROWS)
    hit = iota(shape, int(back)) == unit_rows(iota(shape, 1 - int(back)), single)
    return hit.astype(F32).astype(BF16)


def columns(j):
    return slice(j % 2 * SHARD, (j % 2 + 1) * SHARD)


def by_features(units, rows):
    pick = selection(False, False)
    for unit in range(4):
        value = dot(pick, units[:, unit].reshape(ROWS, SHARD)).astype(BF16)
        for half in range(2):
            j = 4 * half + unit
            rows[j // 2, 0:FOUR, columns(j)] = value[half * FOUR : (half + 1) * FOUR]
    value = dot(selection(True, False), units[:, 4].reshape(ROWS, SHARD)).astype(BF16)
    for j in range(N_MP):
        rows[j // 2, FOUR:, columns(j)] = value[j * GROUPS : (j + 1) * GROUPS]


def by_units(rows, out):
    pick = selection(False, True)
    for unit in range(4):
        halves = [rows[j // 2, 0:FOUR, columns(j)] for j in (unit, 4 + unit)]
        value = dot(pick, jnp.concatenate(halves, axis=0)).astype(BF16)
        out[:, unit] = value.reshape(GROUPS, 8, SHARD)
    eighths = [rows[j // 2, FOUR:, columns(j)] for j in range(N_MP)]
    value = dot(selection(True, True), jnp.concatenate(eighths, axis=0)).astype(BF16)
    out[:, 4] = value.reshape(GROUPS, 8, SHARD)


def slot_codes(shape, dim, chunk):
    index = iota(shape, dim)
    four = lax.shift_right_logical(index, 3) * 16 + (index & 3)
    fifth = lax.shift_right_logical(index - FOUR, 1) * 16 + 4
    return jnp.where(index < FOUR, four, fifth) + chunk * CHUNK


def send_rows(codes, chunk, normed, out, rows):
    slots = slot_codes((SLOTS, TOK), 0, chunk)
    hit = (slots == codes[0:1, :]) | (slots == codes[1:2, :])
    assign = hit.astype(F32).astype(BF16)
    for j in range(N_MP):
        rows[j // 2, :, columns(j)] = dot(assign, normed[j]).astype(BF16)
    by_units(rows, out)


def first_kernel(place, codes, *refs):
    parts, normed, out, rows = refs[:8], refs[8], refs[9], refs[10]
    total = jnp.zeros((TOK, 1), F32)
    for part in parts:
        value = part[0:TOK, :].astype(F32)
        total = total + jnp.sum(value * value, axis=1, keepdims=True)
    scale = lax.rsqrt(total / D + epsilon)
    for other in range(2):
        for step in range(NZ):
            part = parts[other * NZ + step]
            lines = part[TOK : TOK + GAIN_ROWS, :].astype(F32)
            gain = lines[0:1] + lines[1:2] + lines[2:3]
            value = part[0:TOK, :].astype(F32) * scale * gain
            normed[shard_of(place, step, other)] = value.astype(BF16)
    send_rows(codes, 0, normed, out, rows)


def second_kernel(codes, normed, out, rows):
    send_rows(codes, 1, normed, out, rows)


SLAB = (GROUPS, UNITS, 8, SHARD)
SLAB_SHAPE = pltpu.HBM(SLAB, BF16)
ROW_SCRATCH = pltpu.VMEM((NZ, SLOTS, QUARTER), BF16)


def dispatch(place, codes, hidden_state, norm_gain):
    lines = jnp.zeros((GAIN_ROWS, SHARD), F32).at[0:3].set(jnp.stack(terms_of(norm_gain)))
    mine = jnp.concatenate([hidden_state, lines], axis=0).astype(BF16)
    parts = [shift(mine, "z_hi", NZ, step) for step in range(NZ)]
    parts += [swap(value, "core") for value in parts]
    normed, one = call(
        first_kernel,
        (pltpu.HBM((N_MP, TOK, SHARD), BF16), SLAB_SHAPE),
        2_000_000_000,
        6_000_000,
        grid=(1,),
        in_specs=[SMEM, whole((2, TOK))] + [whole((TOK + GAIN_ROWS, SHARD))] * 8,
        out_specs=[whole((N_MP, TOK, SHARD)), whole(SLAB)],
        scratch_shapes=[ROW_SCRATCH],
    )(place, codes, *parts)
    two = call(
        second_kernel,
        SLAB_SHAPE,
        1_000_000_000,
        4_000_000,
        grid=(1,),
        in_specs=[whole((2, TOK)), whole((N_MP, TOK, SHARD))],
        out_specs=whole(SLAB),
        scratch_shapes=[ROW_SCRATCH],
    )(codes, normed)
    return one, two


def terms_of(value):
    first = lax.reduce_precision(value, 8, 7)
    second = lax.reduce_precision(value - first, 8, 7)
    return [first, second, value - first - second]


def load(sources, buffers, sems, cut):
    copies = []
    for q in range(NZ):
        copies.append([])
        for index, source in enumerate(sources):
            copy = pltpu.make_async_copy(source.at[cut(q)], buffers.at[index, q], sems.at[index, q])
            copy.start()
            copies[q].append(copy)
    return copies


def rows_cut(q):
    return pl.ds(q * QUARTER, QUARTER)


def columns_cut(q):
    return slice(None), pl.ds(q * QUARTER, QUARTER)


def experts_kernel(
    units, gate_a, up_a, gate_b, up_b, down_a, down_b, out, rows, gates, downs, sums, active, gate_sems, down_sems
):
    first = load((gate_a, up_a, gate_b, up_b), gates, gate_sems, rows_cut)
    second = load((down_a, down_b), downs, down_sems, columns_cut)
    by_features(units, rows)
    for q in range(NZ):
        for copy in first[q]:
            copy.wait()
        for index in range(4):
            product = dot(rows[q], gates[index, q])
            sums[index] = product if q == 0 else sums[index] + product
    for index in range(2):
        active[index] = (jax.nn.silu(sums[2 * index]) * sums[2 * index + 1]).astype(BF16)
    for q in range(NZ):
        for copy in second[q]:
            copy.wait()
        rows[q] = (dot(active[0], downs[0, q]) + dot(active[1], downs[1, q])).astype(BF16)
    by_units(rows, out)


def experts(arrived, gate, up, down):
    return call(
        experts_kernel,
        SLAB_SHAPE,
        2 * SLOTS * D * HID * 6,
        27_000_000,
        34,
        grid=(1,),
        in_specs=[whole(SLAB)] + [HBM] * 6,
        out_specs=whole(SLAB),
        scratch_shapes=[
            ROW_SCRATCH,
            pltpu.VMEM((4, NZ, QUARTER, HID), BF16),
            pltpu.VMEM((2, NZ, HID, QUARTER), BF16),
            pltpu.VMEM((4, SLOTS, HID), F32),
            pltpu.VMEM((2, SLOTS, HID), BF16),
            pltpu.SemaphoreType.DMA((4, NZ)),
            pltpu.SemaphoreType.DMA((2, NZ)),
        ],
    )(arrived, gate[0], up[0], gate[1], up[1], down[0], down[1])


def combine_kernel(chunk, place, codes, probs, units, keep, give, rows, weights):
    step = pl.program_id(0)

    @pl.when(step == 0)
    def _():
        by_features(units, rows)
        slots = slot_codes((TOK, SLOTS), 1, chunk)
        mixed = jnp.zeros((TOK, SLOTS), F32)
        for choice in range(2):
            hit = slots == codes[:, choice : choice + 1]
            mixed = mixed + jnp.where(hit, probs[:, choice : choice + 1], 0.0)
        upper = mixed.astype(BF16)
        weights[0] = upper
        weights[1] = (mixed - upper.astype(F32)).astype(BF16)

    value = rows[step]
    value = (dot(weights[0], value) + dot(weights[1], value)).astype(BF16)

    @pl.when(place[1] == 0)
    def _():
        keep[0], give[0] = value[:, :SHARD], value[:, SHARD:]

    @pl.when(place[1] == 1)
    def _():
        keep[0], give[0] = value[:, SHARD:], value[:, :SHARD]


def combine_chunk(chunk, place, codes, probs, returned):
    shape = jax.ShapeDtypeStruct((NZ, TOK, SHARD), BF16)
    keep, give = call(
        functools.partial(combine_kernel, chunk),
        (shape, shape),
        2_500_000_000,
        6_000_000,
        grid=(NZ,),
        in_specs=[SMEM, whole((TOK, 2)), whole((TOK, 2)), whole(SLAB)],
        out_specs=[pl.BlockSpec((1, TOK, SHARD), lambda step: (step, 0, 0))] * 2,
        scratch_shapes=[ROW_SCRATCH, pltpu.VMEM((2, TOK, SLOTS), BF16)],
    )(place, codes, probs, returned)
    return keep.astype(F32) + swap(give, "core").astype(F32)


def combine(place, codes, probs, returned):
    early = lax.optimization_barrier(combine_chunk(0, place, codes, probs, returned[0]).astype(BF16))
    both = (combine_chunk(1, place, codes, probs, returned[1]) + early.astype(F32)).astype(BF16)
    total = lax.dynamic_index_in_dim(both, place[0], 0, False).astype(F32)
    for step in range(1, NZ):
        piece = lax.dynamic_index_in_dim(both, lax.rem(place[0] + step, NZ), 0, False)
        total = total + shift(piece, "z_hi", NZ, step).astype(F32)
    return total


def shards(
    attention,
    out_weight,
    residual,
    norm_gain,
    expert_ids,
    slot_index,
    gate_prob,
    w_gate,
    w_up,
    w_down,
):
    place = jnp.stack([lax.axis_index(name) for name in ("z_hi", "core", "z_lo", "x", "y")])
    place = place.astype(jnp.int32)
    slot = slot_index - SHARE * place[1]
    codes = jnp.where((slot_index >= 0) & (slot >= 0) & (slot < SHARE), 16 * expert_ids + slot, -1)

    hidden_state = project(place, attention, out_weight, residual)
    one, two = dispatch(place, codes.T, hidden_state, norm_gain)
    one, gate, up, down = lax.optimization_barrier((one, w_gate[0], w_up[0], w_down[0]))
    gate, up, down = [(value, swap(value, "core")) for value in (gate, up, down)]
    two, gate, up, down = lax.optimization_barrier((two, gate, up, down))
    returned = []
    for rows in (one, two):
        arrived = lax.all_to_all(rows, EXPERT, split_axis=0, concat_axis=0, tiled=True)
        half_out = experts(arrived, gate, up, down)
        returned.append(lax.all_to_all(half_out, EXPERT, split_axis=0, concat_axis=0, tiled=True))
    expert_mix = combine(place, codes, gate_prob, returned)
    return (hidden_state + expert_mix).astype(BF16)


def solution(mesh):
    fine = Mesh(mesh.devices.reshape(SIZES), EXPERT + MP)
    return jax.shard_map(
        shards,
        mesh=fine,
        in_specs=(
            P(EXPERT, MP),
            P(EXPERT, MP),
            P(EXPERT, MP),
            P(MP),
            P(EXPERT, None),
            P(EXPERT, None),
            P(EXPERT, None),
            P(EXPERT, None, MP),
            P(EXPERT, None, MP),
            P(EXPERT, MP, None),
        ),
        out_specs=P(EXPERT, MP),
        check_vma=False,
    )
```

```python
import functools

import jax
import jax.numpy as jnp
from jax import lax
from jax.experimental import pallas as pl
from jax.experimental.pallas import tpu as pltpu
from jax.sharding import Mesh
from jax.sharding import PartitionSpec as P

epsilon = 1e-05

EXPERT = ("z_lo", "y", "x")
MP = ("z_hi", "core")
SIZES = (2, 4, 4, 4, 2)
NX = 4
NY = 4
NZ = 4
N_MP = 8

TOK = 128
D = 7168
SHARD = D // N_MP
FEAT = 448
W_ROWS = 112
GROUPS = 32
HID = 256
SHARE = 10
CHUNK = 5
UNITS = 5
QUARTER = D // NZ
ROWS = GROUPS * 8
FOUR = GROUPS * 4
SLOTS = GROUPS * CHUNK
GAIN_ROWS = 8

BF16 = jnp.bfloat16
F32 = jnp.float32
MIB = 1024 * 1024


def dot(a, b, dims=((1,), (0,))):
    return lax.dot_general(a, b, (dims, ((), ())), preferred_element_type=F32)


def iota(shape, dim):
    return lax.broadcasted_iota(jnp.int32, shape, dim)


def shift(value, axis, size, step):
    if step == 0:
        return value
    return lax.ppermute(value, axis, [(i, (i + step) % size) for i in range(size)])


def swap(value, axis):
    return lax.ppermute(value, axis, [(0, 1), (1, 0)])


def shard_of(place, step, other):
    z = lax.rem(place[0] - step + NZ, NZ)
    core = 1 - place[1] if other else place[1]
    return 2 * z + core


def call(kernel, out_shape, flops, moved, limit=24, **kwargs):
    return pl.pallas_call(
        kernel,
        out_shape=out_shape,
        compiler_params=pltpu.CompilerParams(vmem_limit_bytes=limit * MIB),
        cost_estimate=pl.CostEstimate(flops=flops, bytes_accessed=moved, transcendentals=0),
        **kwargs,
    )


SMEM = pl.BlockSpec(memory_space=pltpu.SMEM)


def whole(shape):
    return pl.BlockSpec(shape, lambda step: (0,) * len(shape))


def project_kernel(place, *refs):
    features, blocks, outs = refs[:8], refs[8:12], refs[12:16]
    rows, weights = refs[16:]
    for other in range(2):
        for step in range(NZ):
            rows[shard_of(place, step, other)] = features[other * NZ + step][...]
    for step in range(NX):
        x = lax.rem(place[3] - step + NX, NX)
        weights[place[2] * NX + x] = blocks[step][0:W_ROWS]
        weights[(1 - place[2]) * NX + x] = blocks[step][W_ROWS:]
    near = weights[0:NX].reshape(FEAT, SHARD)
    later = weights[NX:].reshape(FEAT, SHARD)
    for step, out in enumerate(outs):
        y = lax.rem(place[4] + step, NY)
        total = dot(rows[y], near, ((0,), (0,))) + dot(rows[NY + y], later, ((0,), (0,)))
        out[...] = total.astype(out.dtype)


def project(place, attention, out_weight, residual):
    flipped = attention.T
    features = []
    for step in range(NZ):
        pairs = []
        for y in range(NY):
            for m in range(N_MP):
                z, core = divmod(m // NY * NY + y, 2)
                pairs.append((y * N_MP + m, m % NY * N_MP + (z + step) % NZ * 2 + core))
        features.append(lax.ppermute(flipped, ("y",) + MP, pairs))
    features += [swap(value, "core") for value in features]
    both = jnp.concatenate([out_weight, swap(out_weight, "z_lo")], axis=0)
    blocks = [shift(both, "x", NX, step) for step in range(NX)]
    partial = call(
        project_kernel,
        [jax.ShapeDtypeStruct((TOK, SHARD), BF16 if step else F32) for step in range(NY)],
        2 * NY * TOK * 2 * FEAT * SHARD,
        4_000_000,
        16,
        grid=(1,),
        in_specs=[SMEM] + [whole((FEAT, TOK))] * 8 + [whole((2 * W_ROWS, SHARD))] * 4,
        out_specs=[whole((TOK, SHARD))] * NY,
        scratch_shapes=[
            pltpu.VMEM((N_MP, FEAT, TOK), BF16),
            pltpu.VMEM((2 * NX, W_ROWS, SHARD), BF16),
        ],
    )(place, *features, *blocks)
    total = residual.astype(F32) + partial[0]
    for step in range(1, NY):
        total = total + shift(partial[step], "y", NY, step).astype(F32)
    return total


def unit_rows(index, single):
    group = lax.shift_right_logical(index, 3)
    if single:
        return (index & 7) * GROUPS + group
    return (lax.shift_right_logical(index, 2) & 1) * FOUR + group * 4 + (index & 3)


def selection(single, back):
    shape = (ROWS, ROWS)
    hit = iota(shape, int(back)) == unit_rows(iota(shape, 1 - int(back)), single)
    return hit.astype(F32).astype(BF16)


def columns(j):
    return slice(j % 2 * SHARD, (j % 2 + 1) * SHARD)


def by_features(units, rows):
    pick = selection(False, False)
    for unit in range(4):
        value = dot(pick, units[:, unit].reshape(ROWS, SHARD)).astype(BF16)
        for half in range(2):
            j = 4 * half + unit
            rows[j // 2, 0:FOUR, columns(j)] = value[half * FOUR : (half + 1) * FOUR]
    value = dot(selection(True, False), units[:, 4].reshape(ROWS, SHARD)).astype(BF16)
    for j in range(N_MP):
        rows[j // 2, FOUR:, columns(j)] = value[j * GROUPS : (j + 1) * GROUPS]


def by_units(rows, out):
    pick = selection(False, True)
    for unit in range(4):
        halves = [rows[j // 2, 0:FOUR, columns(j)] for j in (unit, 4 + unit)]
        value = dot(pick, jnp.concatenate(halves, axis=0)).astype(BF16)
        out[:, unit] = value.reshape(GROUPS, 8, SHARD)
    eighths = [rows[j // 2, FOUR:, columns(j)] for j in range(N_MP)]
    value = dot(selection(True, True), jnp.concatenate(eighths, axis=0)).astype(BF16)
    out[:, 4] = value.reshape(GROUPS, 8, SHARD)


def slot_codes(shape, dim, chunk):
    index = iota(shape, dim)
    four = lax.shift_right_logical(index, 3) * 16 + (index & 3)
    fifth = lax.shift_right_logical(index - FOUR, 1) * 16 + 4
    return jnp.where(index < FOUR, four, fifth) + chunk * CHUNK


def send_rows(codes, chunk, normed, out, rows):
    slots = slot_codes((SLOTS, TOK), 0, chunk)
    hit = (slots == codes[0:1, :]) | (slots == codes[1:2, :])
    assign = hit.astype(F32).astype(BF16)
    for j in range(N_MP):
        rows[j // 2, :, columns(j)] = dot(assign, normed[j]).astype(BF16)
    by_units(rows, out)


def first_kernel(place, codes, *refs):
    parts, normed, out, rows = refs[:8], refs[8], refs[9], refs[10]
    total = jnp.zeros((TOK, 1), F32)
    for part in parts:
        value = part[...].astype(F32)[0:TOK]
        total = total + jnp.sum(value * value, axis=1, keepdims=True)
    scale = lax.rsqrt(total / D + epsilon)
    for other in range(2):
        for step in range(NZ):
            lines = parts[other * NZ + step][...].astype(F32)
            gain = lines[TOK : TOK + 1] + lines[TOK + 1 : TOK + 2] + lines[TOK + 2 : TOK + 3]
            value = lines[0:TOK] * scale * gain
            normed[shard_of(place, step, other)] = value.astype(BF16)
    send_rows(codes, 0, normed, out, rows)


def second_kernel(codes, normed, out, rows):
    send_rows(codes, 1, normed, out, rows)


SLAB = (GROUPS, UNITS, 8, SHARD)
SLAB_SHAPE = pltpu.HBM(SLAB, BF16)
ROW_SCRATCH = pltpu.VMEM((NZ, SLOTS, QUARTER), BF16)


def dispatch(place, codes, hidden_state, norm_gain):
    lines = jnp.zeros((GAIN_ROWS, SHARD), F32).at[0:3].set(jnp.stack(terms_of(norm_gain)))
    mine = jnp.concatenate([hidden_state, lines], axis=0).astype(BF16)
    parts = [shift(mine, "z_hi", NZ, step) for step in range(NZ)]
    parts += [swap(value, "core") for value in parts]
    normed, one = call(
        first_kernel,
        (pltpu.HBM((N_MP, TOK, SHARD), BF16), SLAB_SHAPE),
        2_000_000_000,
        6_000_000,
        grid=(1,),
        in_specs=[SMEM, whole((2, TOK))] + [whole((TOK + GAIN_ROWS, SHARD))] * 8,
        out_specs=[whole((N_MP, TOK, SHARD)), whole(SLAB)],
        scratch_shapes=[ROW_SCRATCH],
    )(place, codes, *parts)
    two = call(
        second_kernel,
        SLAB_SHAPE,
        1_000_000_000,
        4_000_000,
        grid=(1,),
        in_specs=[whole((2, TOK)), whole((N_MP, TOK, SHARD))],
        out_specs=whole(SLAB),
        scratch_shapes=[ROW_SCRATCH],
    )(codes, normed)
    return one, two


def terms_of(value):
    first = lax.reduce_precision(value, 8, 7)
    second = lax.reduce_precision(value - first, 8, 7)
    return [first, second, value - first - second]


def experts_kernel(units, gate_a, up_a, gate_b, up_b, down_a, down_b, out, rows, sums, active):
    step = pl.program_id(0)

    @pl.when(step == 0)
    def _():
        by_features(units, rows)
        sums[...] = jnp.zeros_like(sums)

    @pl.when(step < NZ)
    def _():
        for index, weight in enumerate((gate_a, up_a, gate_b, up_b)):
            sums[index] = sums[index] + dot(rows[step], weight[...])

    @pl.when(step == NZ)
    def _():
        for index in range(2):
            active[index] = (jax.nn.silu(sums[2 * index]) * sums[2 * index + 1]).astype(BF16)

    @pl.when(step >= NZ)
    def _():
        rows[step - NZ] = (dot(active[0], down_a[...]) + dot(active[1], down_b[...])).astype(BF16)

    @pl.when(step == 2 * NZ - 1)
    def _():
        by_units(rows, out)


def experts(arrived, gate, up, down):
    first = lambda step: (jnp.minimum(step, NZ - 1), 0)
    second = lambda step: (0, jnp.maximum(step - NZ, 0))
    return call(
        experts_kernel,
        SLAB_SHAPE,
        2 * SLOTS * D * HID * 6,
        27_000_000,
        34,
        grid=(2 * NZ,),
        in_specs=[whole(SLAB)]
        + [pl.BlockSpec((QUARTER, HID), first)] * 4
        + [pl.BlockSpec((HID, QUARTER), second)] * 2,
        out_specs=whole(SLAB),
        scratch_shapes=[
            ROW_SCRATCH,
            pltpu.VMEM((4, SLOTS, HID), F32),
            pltpu.VMEM((2, SLOTS, HID), BF16),
        ],
    )(arrived, gate[0], up[0], gate[1], up[1], down[0], down[1])


def combine_kernel(chunk, place, codes, probs, units, keep, give, rows, weights):
    step = pl.program_id(0)

    @pl.when(step == 0)
    def _():
        by_features(units, rows)
        slots = slot_codes((TOK, SLOTS), 1, chunk)
        mixed = jnp.zeros((TOK, SLOTS), F32)
        for choice in range(2):
            hit = slots == codes[:, choice : choice + 1]
            mixed = mixed + jnp.where(hit, probs[:, choice : choice + 1], 0.0)
        upper = mixed.astype(BF16)
        weights[0] = upper
        weights[1] = (mixed - upper.astype(F32)).astype(BF16)

    value = rows[step]
    value = (dot(weights[0], value) + dot(weights[1], value)).astype(BF16)

    @pl.when(place[1] == 0)
    def _():
        keep[0], give[0] = value[:, :SHARD], value[:, SHARD:]

    @pl.when(place[1] == 1)
    def _():
        keep[0], give[0] = value[:, SHARD:], value[:, :SHARD]


def combine_chunk(chunk, place, codes, probs, returned):
    shape = jax.ShapeDtypeStruct((NZ, TOK, SHARD), BF16)
    keep, give = call(
        functools.partial(combine_kernel, chunk),
        (shape, shape),
        2_500_000_000,
        6_000_000,
        grid=(NZ,),
        in_specs=[SMEM, whole((TOK, 2)), whole((TOK, 2)), whole(SLAB)],
        out_specs=[pl.BlockSpec((1, TOK, SHARD), lambda step: (step, 0, 0))] * 2,
        scratch_shapes=[ROW_SCRATCH, pltpu.VMEM((2, TOK, SLOTS), BF16)],
    )(place, codes, probs, returned)
    return keep.astype(F32) + swap(give, "core").astype(F32)


def combine(place, codes, probs, returned):
    early = lax.optimization_barrier(combine_chunk(0, place, codes, probs, returned[0]).astype(BF16))
    both = (combine_chunk(1, place, codes, probs, returned[1]) + early.astype(F32)).astype(BF16)
    total = lax.dynamic_index_in_dim(both, place[0], 0, False).astype(F32)
    for step in range(1, NZ):
        piece = lax.dynamic_index_in_dim(both, lax.rem(place[0] + step, NZ), 0, False)
        total = total + shift(piece, "z_hi", NZ, step).astype(F32)
    return total


def shards(
    attention,
    out_weight,
    residual,
    norm_gain,
    expert_ids,
    slot_index,
    gate_prob,
    w_gate,
    w_up,
    w_down,
):
    place = jnp.stack([lax.axis_index(name) for name in ("z_hi", "core", "z_lo", "x", "y")])
    place = place.astype(jnp.int32)
    slot = slot_index - SHARE * place[1]
    codes = jnp.where((slot_index >= 0) & (slot >= 0) & (slot < SHARE), 16 * expert_ids + slot, -1)

    hidden_state = project(place, attention, out_weight, residual)
    one, two = dispatch(place, codes.T, hidden_state, norm_gain)
    one, gate, up, down = lax.optimization_barrier((one, w_gate[0], w_up[0], w_down[0]))
    gate, up, down = [(value, swap(value, "core")) for value in (gate, up, down)]
    two, gate, up, down = lax.optimization_barrier((two, gate, up, down))
    returned = []
    for rows in (one, two):
        arrived = lax.all_to_all(rows, EXPERT, split_axis=0, concat_axis=0, tiled=True)
        half_out = experts(arrived, gate, up, down)
        returned.append(lax.all_to_all(half_out, EXPERT, split_axis=0, concat_axis=0, tiled=True))
    expert_mix = combine(place, codes, gate_prob, returned)
    return (hidden_state + expert_mix).astype(BF16)


def solution(mesh):
    fine = Mesh(mesh.devices.reshape(SIZES), EXPERT + MP)
    return jax.shard_map(
        shards,
        mesh=fine,
        in_specs=(
            P(EXPERT, MP),
            P(EXPERT, MP),
            P(EXPERT, MP),
            P(MP),
            P(EXPERT, None),
            P(EXPERT, None),
            P(EXPERT, None),
            P(EXPERT, None, MP),
            P(EXPERT, None, MP),
            P(EXPERT, MP, None),
        ),
        out_specs=P(EXPERT, MP),
        check_vma=False,
    )
```

```python
import functools

import jax
import jax.numpy as jnp
from jax import lax
from jax.experimental import pallas as pl
from jax.experimental.pallas import tpu as pltpu
from jax.sharding import Mesh
from jax.sharding import PartitionSpec as P

epsilon = 1e-05

EXPERT = ("z_lo", "y", "x")
MP = ("z_hi", "core")
SIZES = (2, 4, 4, 4, 2)
NX = 4
NY = 4
NZ = 4
N_MP = 8

TOK = 128
D = 7168
SHARD = D // N_MP
FEAT = 448
W_ROWS = 112
GROUPS = 32
HID = 256
SHARE = 10
CHUNK = 5
UNITS = 5
QUARTER = D // NZ
ROWS = GROUPS * 8
FOUR = GROUPS * 4
SLOTS = GROUPS * CHUNK
GAIN_ROWS = 8

BF16 = jnp.bfloat16
F32 = jnp.float32
MIB = 1024 * 1024


def dot(a, b, dims=((1,), (0,))):
    return lax.dot_general(a, b, (dims, ((), ())), preferred_element_type=F32)


def iota(shape, dim):
    return lax.broadcasted_iota(jnp.int32, shape, dim)


def shift(value, axis, size, step):
    if step == 0:
        return value
    return lax.ppermute(value, axis, [(i, (i + step) % size) for i in range(size)])


def swap(value, axis):
    return lax.ppermute(value, axis, [(0, 1), (1, 0)])


def shard_of(place, step, other):
    z = lax.rem(place[0] - step + NZ, NZ)
    core = 1 - place[1] if other else place[1]
    return 2 * z + core


def call(kernel, out_shape, flops, moved, limit=24, **kwargs):
    return pl.pallas_call(
        kernel,
        out_shape=out_shape,
        compiler_params=pltpu.CompilerParams(vmem_limit_bytes=limit * MIB),
        cost_estimate=pl.CostEstimate(flops=flops, bytes_accessed=moved, transcendentals=0),
        **kwargs,
    )


SMEM = pl.BlockSpec(memory_space=pltpu.SMEM)


def whole(shape):
    return pl.BlockSpec(shape, lambda step: (0,) * len(shape))


def project_kernel(place, *refs):
    features, blocks, outs = refs[:8], refs[8:12], refs[12:16]
    rows, weights = refs[16:]
    for other in range(2):
        for step in range(NZ):
            rows[shard_of(place, step, other)] = features[other * NZ + step][...]
    for step in range(NX):
        x = lax.rem(place[3] - step + NX, NX)
        weights[place[2] * NX + x] = blocks[step][0:W_ROWS]
        weights[(1 - place[2]) * NX + x] = blocks[step][W_ROWS:]
    near = weights[0:NX].reshape(FEAT, SHARD)
    later = weights[NX:].reshape(FEAT, SHARD)
    for step, out in enumerate(outs):
        y = lax.rem(place[4] + step, NY)
        total = dot(rows[y], near, ((0,), (0,))) + dot(rows[NY + y], later, ((0,), (0,)))
        out[...] = total.astype(out.dtype)


def project(place, attention, out_weight, residual):
    flipped = attention.T
    features = []
    for step in range(NZ):
        pairs = []
        for y in range(NY):
            for m in range(N_MP):
                z, core = divmod(m // NY * NY + y, 2)
                pairs.append((y * N_MP + m, m % NY * N_MP + (z + step) % NZ * 2 + core))
        features.append(lax.ppermute(flipped, ("y",) + MP, pairs))
    features += [swap(value, "core") for value in features]
    both = jnp.concatenate([out_weight, swap(out_weight, "z_lo")], axis=0)
    blocks = [shift(both, "x", NX, step) for step in range(NX)]
    partial = call(
        project_kernel,
        [jax.ShapeDtypeStruct((TOK, SHARD), BF16 if step else F32) for step in range(NY)],
        2 * NY * TOK * 2 * FEAT * SHARD,
        4_000_000,
        16,
        grid=(1,),
        in_specs=[SMEM] + [whole((FEAT, TOK))] * 8 + [whole((2 * W_ROWS, SHARD))] * 4,
        out_specs=[whole((TOK, SHARD))] * NY,
        scratch_shapes=[
            pltpu.VMEM((N_MP, FEAT, TOK), BF16),
            pltpu.VMEM((2 * NX, W_ROWS, SHARD), BF16),
        ],
    )(place, *features, *blocks)
    total = residual.astype(F32) + partial[0]
    for step in range(1, NY):
        total = total + shift(partial[step], "y", NY, step).astype(F32)
    return total


def unit_rows(index, single):
    group = lax.shift_right_logical(index, 3)
    if single:
        return (index & 7) * GROUPS + group
    return (lax.shift_right_logical(index, 2) & 1) * FOUR + group * 4 + (index & 3)


def selection(single, back):
    shape = (ROWS, ROWS)
    hit = iota(shape, int(back)) == unit_rows(iota(shape, 1 - int(back)), single)
    return hit.astype(F32).astype(BF16)


def columns(j):
    return slice(j % 2 * SHARD, (j % 2 + 1) * SHARD)


def by_features(units, rows):
    pick = selection(False, False)
    for unit in range(4):
        value = dot(pick, units[:, unit].reshape(ROWS, SHARD)).astype(BF16)
        for half in range(2):
            j = 4 * half + unit
            rows[j // 2, 0:FOUR, columns(j)] = value[half * FOUR : (half + 1) * FOUR]
    value = dot(selection(True, False), units[:, 4].reshape(ROWS, SHARD)).astype(BF16)
    for j in range(N_MP):
        rows[j // 2, FOUR:, columns(j)] = value[j * GROUPS : (j + 1) * GROUPS]


def by_units(rows, out):
    pick = selection(False, True)
    for unit in range(4):
        halves = [rows[j // 2, 0:FOUR, columns(j)] for j in (unit, 4 + unit)]
        value = dot(pick, jnp.concatenate(halves, axis=0)).astype(BF16)
        out[:, unit] = value.reshape(GROUPS, 8, SHARD)
    eighths = [rows[j // 2, FOUR:, columns(j)] for j in range(N_MP)]
    value = dot(selection(True, True), jnp.concatenate(eighths, axis=0)).astype(BF16)
    out[:, 4] = value.reshape(GROUPS, 8, SHARD)


def slot_codes(shape, dim, chunk):
    index = iota(shape, dim)
    four = lax.shift_right_logical(index, 3) * 16 + (index & 3)
    fifth = lax.shift_right_logical(index - FOUR, 1) * 16 + 4
    return jnp.where(index < FOUR, four, fifth) + chunk * CHUNK


def send_rows(codes, chunk, normed, out, rows):
    slots = slot_codes((SLOTS, TOK), 0, chunk)
    hit = (slots == codes[0:1, :]) | (slots == codes[1:2, :])
    assign = hit.astype(F32).astype(BF16)
    for j in range(N_MP):
        rows[j // 2, :, columns(j)] = dot(assign, normed[j]).astype(BF16)
    by_units(rows, out)


def first_kernel(place, codes, *refs):
    parts, normed, out, rows = refs[:8], refs[8], refs[9], refs[10]
    total = jnp.zeros((TOK, 1), F32)
    for part in parts:
        value = part[...].astype(F32)[0:TOK]
        total = total + jnp.sum(value * value, axis=1, keepdims=True)
    scale = lax.rsqrt(total / D + epsilon)
    for other in range(2):
        for step in range(NZ):
            lines = parts[other * NZ + step][...].astype(F32)
            gain = lines[TOK : TOK + 1] + lines[TOK + 1 : TOK + 2] + lines[TOK + 2 : TOK + 3]
            value = lines[0:TOK] * scale * gain
            normed[shard_of(place, step, other)] = value.astype(BF16)
    send_rows(codes, 0, normed, out, rows)


def second_kernel(codes, normed, out, rows):
    send_rows(codes, 1, normed, out, rows)


SLAB = (GROUPS, UNITS, 8, SHARD)
SLAB_SHAPE = pltpu.HBM(SLAB, BF16)
ROW_SCRATCH = pltpu.VMEM((NZ, SLOTS, QUARTER), BF16)


def dispatch(place, codes, hidden_state, norm_gain):
    lines = jnp.zeros((GAIN_ROWS, SHARD), F32).at[0:3].set(jnp.stack(terms_of(norm_gain)))
    mine = jnp.concatenate([hidden_state, lines], axis=0).astype(BF16)
    parts = [shift(mine, "z_hi", NZ, step) for step in range(NZ)]
    parts += [swap(value, "core") for value in parts]
    normed, one = call(
        first_kernel,
        (pltpu.HBM((N_MP, TOK, SHARD), BF16), SLAB_SHAPE),
        2_000_000_000,
        6_000_000,
        grid=(1,),
        in_specs=[SMEM, whole((2, TOK))] + [whole((TOK + GAIN_ROWS, SHARD))] * 8,
        out_specs=[whole((N_MP, TOK, SHARD)), whole(SLAB)],
        scratch_shapes=[ROW_SCRATCH],
    )(place, codes, *parts)
    two = call(
        second_kernel,
        SLAB_SHAPE,
        1_000_000_000,
        4_000_000,
        grid=(1,),
        in_specs=[whole((2, TOK)), whole((N_MP, TOK, SHARD))],
        out_specs=whole(SLAB),
        scratch_shapes=[ROW_SCRATCH],
    )(codes, normed)
    return one, two


def terms_of(value):
    first = lax.reduce_precision(value, 8, 7)
    second = lax.reduce_precision(value - first, 8, 7)
    return [first, second, value - first - second]


def experts_kernel(units, gate_a, up_a, gate_b, up_b, down_a, down_b, out, rows, sums, active):
    step = pl.program_id(0)

    @pl.when(step == 0)
    def _():
        by_features(units, rows)
        sums[...] = jnp.zeros_like(sums)

    @pl.when(step < NZ)
    def _():
        for index, weight in enumerate((gate_a, up_a, gate_b, up_b)):
            sums[index] = sums[index] + dot(rows[step], weight[...])

    @pl.when(step == NZ)
    def _():
        for index in range(2):
            active[index] = (jax.nn.silu(sums[2 * index]) * sums[2 * index + 1]).astype(BF16)

    @pl.when(step >= NZ)
    def _():
        rows[step - NZ] = (dot(active[0], down_a[...]) + dot(active[1], down_b[...])).astype(BF16)

    @pl.when(step == 2 * NZ - 1)
    def _():
        by_units(rows, out)


def experts(arrived, gate, up, down):
    first = lambda step: (jnp.minimum(step, NZ - 1), 0)
    second = lambda step: (0, jnp.maximum(step - NZ, 0))
    return call(
        experts_kernel,
        SLAB_SHAPE,
        2 * SLOTS * D * HID * 6,
        27_000_000,
        34,
        grid=(2 * NZ,),
        in_specs=[whole(SLAB)]
        + [pl.BlockSpec((QUARTER, HID), first)] * 4
        + [pl.BlockSpec((HID, QUARTER), second)] * 2,
        out_specs=whole(SLAB),
        scratch_shapes=[
            ROW_SCRATCH,
            pltpu.VMEM((4, SLOTS, HID), F32),
            pltpu.VMEM((2, SLOTS, HID), BF16),
        ],
    )(arrived, gate[0], up[0], gate[1], up[1], down[0], down[1])


def combine_kernel(chunk, place, codes, probs, units, keep, give, rows, weights):
    step = pl.program_id(0)

    @pl.when(step == 0)
    def _():
        by_features(units, rows)
        slots = slot_codes((TOK, SLOTS), 1, chunk)
        mixed = jnp.zeros((TOK, SLOTS), F32)
        for choice in range(2):
            hit = slots == codes[:, choice : choice + 1]
            mixed = mixed + jnp.where(hit, probs[:, choice : choice + 1], 0.0)
        upper = mixed.astype(BF16)
        weights[0] = upper
        weights[1] = (mixed - upper.astype(F32)).astype(BF16)

    value = rows[step]
    value = (dot(weights[0], value) + dot(weights[1], value)).astype(BF16)

    @pl.when(place[1] == 0)
    def _():
        keep[0], give[0] = value[:, :SHARD], value[:, SHARD:]

    @pl.when(place[1] == 1)
    def _():
        keep[0], give[0] = value[:, SHARD:], value[:, :SHARD]


def combine_chunk(chunk, place, codes, probs, returned):
    shape = jax.ShapeDtypeStruct((NZ, TOK, SHARD), BF16)
    keep, give = call(
        functools.partial(combine_kernel, chunk),
        (shape, shape),
        2_500_000_000,
        6_000_000,
        14,
        grid=(NZ,),
        in_specs=[SMEM, whole((TOK, 2)), whole((TOK, 2)), whole(SLAB)],
        out_specs=[pl.BlockSpec((1, TOK, SHARD), lambda step: (step, 0, 0))] * 2,
        scratch_shapes=[ROW_SCRATCH, pltpu.VMEM((2, TOK, SLOTS), BF16)],
    )(place, codes, probs, returned)
    return keep.astype(F32) + swap(give, "core").astype(F32)


def combine(place, codes, probs, returned):
    early = lax.optimization_barrier(combine_chunk(0, place, codes, probs, returned[0]).astype(BF16))
    both = (combine_chunk(1, place, codes, probs, returned[1]) + early.astype(F32)).astype(BF16)
    total = lax.dynamic_index_in_dim(both, place[0], 0, False).astype(F32)
    for step in range(1, NZ):
        piece = lax.dynamic_index_in_dim(both, lax.rem(place[0] + step, NZ), 0, False)
        total = total + shift(piece, "z_hi", NZ, step).astype(F32)
    return total


def shards(
    attention,
    out_weight,
    residual,
    norm_gain,
    expert_ids,
    slot_index,
    gate_prob,
    w_gate,
    w_up,
    w_down,
):
    place = jnp.stack([lax.axis_index(name) for name in ("z_hi", "core", "z_lo", "x", "y")])
    place = place.astype(jnp.int32)
    slot = slot_index - SHARE * place[1]
    codes = jnp.where((slot_index >= 0) & (slot >= 0) & (slot < SHARE), 16 * expert_ids + slot, -1)

    hidden_state = project(place, attention, out_weight, residual)
    one, two = dispatch(place, codes.T, hidden_state, norm_gain)
    one, hidden_state, gate, up, down = lax.optimization_barrier(
        (one, hidden_state, w_gate[0], w_up[0], w_down[0])
    )
    gate, up, down = [(value, swap(value, "core")) for value in (gate, up, down)]
    two, gate, up, down = lax.optimization_barrier((two, gate, up, down))
    returned = []
    for rows in (one, two):
        arrived = lax.all_to_all(rows, EXPERT, split_axis=0, concat_axis=0, tiled=True)
        half_out = experts(arrived, gate, up, down)
        returned.append(lax.all_to_all(half_out, EXPERT, split_axis=0, concat_axis=0, tiled=True))
    expert_mix = combine(place, codes, gate_prob, returned)
    return (hidden_state + expert_mix).astype(BF16)


def solution(mesh):
    fine = Mesh(mesh.devices.reshape(SIZES), EXPERT + MP)
    return jax.shard_map(
        shards,
        mesh=fine,
        in_specs=(
            P(EXPERT, MP),
            P(EXPERT, MP),
            P(EXPERT, MP),
            P(MP),
            P(EXPERT, None),
            P(EXPERT, None),
            P(EXPERT, None),
            P(EXPERT, None, MP),
            P(EXPERT, None, MP),
            P(EXPERT, MP, None),
        ),
        out_specs=P(EXPERT, MP),
        check_vma=False,
    )
```

```python
import functools

import jax
import jax.numpy as jnp
from jax import lax
from jax.experimental import pallas as pl
from jax.experimental.pallas import tpu as pltpu
from jax.sharding import Mesh
from jax.sharding import PartitionSpec as P

epsilon = 1e-05

EXPERT = ("z_lo", "y", "x")
MP = ("z_hi", "core")
SIZES = (2, 4, 4, 4, 2)
NX = 4
NY = 4
NZ = 4
N_MP = 8

TOK = 128
D = 7168
SHARD = D // N_MP
FEAT = 448
W_ROWS = 112
GROUPS = 32
HID = 256
SHARE = 10
CHUNK = 5
UNITS = 5
QUARTER = D // NZ
ROWS = GROUPS * 8
FOUR = GROUPS * 4
SLOTS = GROUPS * CHUNK
GAIN_ROWS = 8

BF16 = jnp.bfloat16
F32 = jnp.float32
MIB = 1024 * 1024


def dot(a, b, dims=((1,), (0,))):
    return lax.dot_general(a, b, (dims, ((), ())), preferred_element_type=F32)


def iota(shape, dim):
    return lax.broadcasted_iota(jnp.int32, shape, dim)


def shift(value, axis, size, step):
    if step == 0:
        return value
    return lax.ppermute(value, axis, [(i, (i + step) % size) for i in range(size)])


def swap(value, axis):
    return lax.ppermute(value, axis, [(0, 1), (1, 0)])


def shard_of(place, step, other):
    z = lax.rem(place[0] - step + NZ, NZ)
    core = 1 - place[1] if other else place[1]
    return 2 * z + core


def call(kernel, out_shape, flops, moved, limit=24, **kwargs):
    return pl.pallas_call(
        kernel,
        out_shape=out_shape,
        compiler_params=pltpu.CompilerParams(vmem_limit_bytes=limit * MIB),
        cost_estimate=pl.CostEstimate(flops=flops, bytes_accessed=moved, transcendentals=0),
        **kwargs,
    )


SMEM = pl.BlockSpec(memory_space=pltpu.SMEM)


def whole(shape):
    return pl.BlockSpec(shape, lambda step: (0,) * len(shape))


def project_kernel(place, *refs):
    features, blocks, outs = refs[:8], refs[8:12], refs[12:16]
    rows, weights = refs[16:]
    for other in range(2):
        for step in range(NZ):
            rows[shard_of(place, step, other)] = features[other * NZ + step][...]
    for step in range(NX):
        x = lax.rem(place[3] - step + NX, NX)
        weights[place[2] * NX + x] = blocks[step][0:W_ROWS]
        weights[(1 - place[2]) * NX + x] = blocks[step][W_ROWS:]
    near = weights[0:NX].reshape(FEAT, SHARD)
    later = weights[NX:].reshape(FEAT, SHARD)
    for step, out in enumerate(outs):
        y = lax.rem(place[4] + step, NY)
        total = dot(rows[y], near, ((0,), (0,))) + dot(rows[NY + y], later, ((0,), (0,)))
        out[...] = total.astype(out.dtype)


def project(place, attention, out_weight, residual):
    flipped = attention.T
    features = []
    for step in range(NZ):
        pairs = []
        for y in range(NY):
            for m in range(N_MP):
                z, core = divmod(m // NY * NY + y, 2)
                pairs.append((y * N_MP + m, m % NY * N_MP + (z + step) % NZ * 2 + core))
        features.append(lax.ppermute(flipped, ("y",) + MP, pairs))
    features += [swap(value, "core") for value in features]
    both = jnp.concatenate([out_weight, swap(out_weight, "z_lo")], axis=0)
    blocks = [shift(both, "x", NX, step) for step in range(NX)]
    partial = call(
        project_kernel,
        [jax.ShapeDtypeStruct((TOK, SHARD), BF16 if step else F32) for step in range(NY)],
        2 * NY * TOK * 2 * FEAT * SHARD,
        4_000_000,
        16,
        grid=(1,),
        in_specs=[SMEM] + [whole((FEAT, TOK))] * 8 + [whole((2 * W_ROWS, SHARD))] * 4,
        out_specs=[whole((TOK, SHARD))] * NY,
        scratch_shapes=[
            pltpu.VMEM((N_MP, FEAT, TOK), BF16),
            pltpu.VMEM((2 * NX, W_ROWS, SHARD), BF16),
        ],
    )(place, *features, *blocks)
    total = residual.astype(F32) + partial[0]
    for step in range(1, NY):
        total = total + shift(partial[step], "y", NY, step).astype(F32)
    return total


def unit_rows(index, single):
    group = lax.shift_right_logical(index, 3)
    if single:
        return (index & 7) * GROUPS + group
    return (lax.shift_right_logical(index, 2) & 1) * FOUR + group * 4 + (index & 3)


def selection(single, back):
    shape = (ROWS, ROWS)
    hit = iota(shape, int(back)) == unit_rows(iota(shape, 1 - int(back)), single)
    return hit.astype(F32).astype(BF16)


def columns(j):
    return slice(j % 2 * SHARD, (j % 2 + 1) * SHARD)


def by_features(units, rows):
    pick = selection(False, False)
    for unit in range(4):
        value = dot(pick, units[:, unit].reshape(ROWS, SHARD)).astype(BF16)
        for half in range(2):
            j = 4 * half + unit
            rows[j // 2, 0:FOUR, columns(j)] = value[half * FOUR : (half + 1) * FOUR]
    value = dot(selection(True, False), units[:, 4].reshape(ROWS, SHARD)).astype(BF16)
    for j in range(N_MP):
        rows[j // 2, FOUR:, columns(j)] = value[j * GROUPS : (j + 1) * GROUPS]


def by_units(rows, out):
    pick = selection(False, True)
    for unit in range(4):
        halves = [rows[j // 2, 0:FOUR, columns(j)] for j in (unit, 4 + unit)]
        value = dot(pick, jnp.concatenate(halves, axis=0)).astype(BF16)
        out[:, unit] = value.reshape(GROUPS, 8, SHARD)
    eighths = [rows[j // 2, FOUR:, columns(j)] for j in range(N_MP)]
    value = dot(selection(True, True), jnp.concatenate(eighths, axis=0)).astype(BF16)
    out[:, 4] = value.reshape(GROUPS, 8, SHARD)


def slot_codes(shape, dim, chunk):
    index = iota(shape, dim)
    four = lax.shift_right_logical(index, 3) * 16 + (index & 3)
    fifth = lax.shift_right_logical(index - FOUR, 1) * 16 + 4
    return jnp.where(index < FOUR, four, fifth) + chunk * CHUNK


def send_rows(codes, chunk, normed, out, rows):
    slots = slot_codes((SLOTS, TOK), 0, chunk)
    hit = (slots == codes[0:1, :]) | (slots == codes[1:2, :])
    assign = hit.astype(F32).astype(BF16)
    for j in range(N_MP):
        rows[j // 2, :, columns(j)] = dot(assign, normed[j]).astype(BF16)
    by_units(rows, out)


def first_kernel(place, codes, *refs):
    parts, normed, out, rows = refs[:8], refs[8], refs[9], refs[10]
    total = jnp.zeros((TOK, 1), F32)
    for part in parts:
        value = part[...].astype(F32)[0:TOK]
        total = total + jnp.sum(value * value, axis=1, keepdims=True)
    scale = lax.rsqrt(total / D + epsilon)
    for other in range(2):
        for step in range(NZ):
            lines = parts[other * NZ + step][...].astype(F32)
            gain = lines[TOK : TOK + 1] + lines[TOK + 1 : TOK + 2] + lines[TOK + 2 : TOK + 3]
            value = lines[0:TOK] * scale * gain
            normed[shard_of(place, step, other)] = value.astype(BF16)
    send_rows(codes, 0, normed, out, rows)


def second_kernel(codes, normed, out, rows):
    send_rows(codes, 1, normed, out, rows)


SLAB = (GROUPS, UNITS, 8, SHARD)
SLAB_SHAPE = pltpu.HBM(SLAB, BF16)
ROW_SCRATCH = pltpu.VMEM((NZ, SLOTS, QUARTER), BF16)


def dispatch(place, codes, hidden_state, norm_gain):
    lines = jnp.zeros((GAIN_ROWS, SHARD), F32).at[0:3].set(jnp.stack(terms_of(norm_gain)))
    mine = jnp.concatenate([hidden_state, lines], axis=0).astype(BF16)
    parts = [shift(mine, "z_hi", NZ, step) for step in range(NZ)]
    parts += [swap(value, "core") for value in parts]
    normed, one = call(
        first_kernel,
        (jax.ShapeDtypeStruct((N_MP, TOK, SHARD), BF16), SLAB_SHAPE),
        2_000_000_000,
        6_000_000,
        grid=(1,),
        in_specs=[SMEM, whole((2, TOK))] + [whole((TOK + GAIN_ROWS, SHARD))] * 8,
        out_specs=[whole((N_MP, TOK, SHARD)), whole(SLAB)],
        scratch_shapes=[ROW_SCRATCH],
    )(place, codes, *parts)
    two = call(
        second_kernel,
        SLAB_SHAPE,
        1_000_000_000,
        4_000_000,
        grid=(1,),
        in_specs=[whole((2, TOK)), whole((N_MP, TOK, SHARD))],
        out_specs=whole(SLAB),
        scratch_shapes=[ROW_SCRATCH],
    )(codes, normed)
    return one, two


def terms_of(value):
    first = lax.reduce_precision(value, 8, 7)
    second = lax.reduce_precision(value - first, 8, 7)
    return [first, second, value - first - second]


def experts_kernel(units, gate_a, up_a, gate_b, up_b, down_a, down_b, out, rows, sums, active):
    step = pl.program_id(0)

    @pl.when(step == 0)
    def _():
        by_features(units, rows)
        sums[...] = jnp.zeros_like(sums)

    @pl.when(step < NZ)
    def _():
        for index, weight in enumerate((gate_a, up_a, gate_b, up_b)):
            sums[index] = sums[index] + dot(rows[step], weight[...])

    @pl.when(step == NZ)
    def _():
        for index in range(2):
            active[index] = (jax.nn.silu(sums[2 * index]) * sums[2 * index + 1]).astype(BF16)

    @pl.when(step >= NZ)
    def _():
        rows[step - NZ] = (dot(active[0], down_a[...]) + dot(active[1], down_b[...])).astype(BF16)

    @pl.when(step == 2 * NZ - 1)
    def _():
        by_units(rows, out)


def experts(arrived, gate, up, down):
    first = lambda step: (jnp.minimum(step, NZ - 1), 0)
    second = lambda step: (0, jnp.maximum(step - NZ, 0))
    return call(
        experts_kernel,
        SLAB_SHAPE,
        2 * SLOTS * D * HID * 6,
        27_000_000,
        34,
        grid=(2 * NZ,),
        in_specs=[whole(SLAB)]
        + [pl.BlockSpec((QUARTER, HID), first)] * 4
        + [pl.BlockSpec((HID, QUARTER), second)] * 2,
        out_specs=whole(SLAB),
        scratch_shapes=[
            ROW_SCRATCH,
            pltpu.VMEM((4, SLOTS, HID), F32),
            pltpu.VMEM((2, SLOTS, HID), BF16),
        ],
    )(arrived, gate[0], up[0], gate[1], up[1], down[0], down[1])


def combine_kernel(chunk, place, codes, probs, units, keep, give, rows, weights):
    step = pl.program_id(0)

    @pl.when(step == 0)
    def _():
        by_features(units, rows)
        slots = slot_codes((TOK, SLOTS), 1, chunk)
        mixed = jnp.zeros((TOK, SLOTS), F32)
        for choice in range(2):
            hit = slots == codes[:, choice : choice + 1]
            mixed = mixed + jnp.where(hit, probs[:, choice : choice + 1], 0.0)
        upper = mixed.astype(BF16)
        weights[0] = upper
        weights[1] = (mixed - upper.astype(F32)).astype(BF16)

    value = rows[step]
    value = (dot(weights[0], value) + dot(weights[1], value)).astype(BF16)

    @pl.when(place[1] == 0)
    def _():
        keep[0], give[0] = value[:, :SHARD], value[:, SHARD:]

    @pl.when(place[1] == 1)
    def _():
        keep[0], give[0] = value[:, SHARD:], value[:, :SHARD]


def combine_chunk(chunk, place, codes, probs, returned):
    shape = jax.ShapeDtypeStruct((NZ, TOK, SHARD), BF16)
    keep, give = call(
        functools.partial(combine_kernel, chunk),
        (shape, shape),
        2_500_000_000,
        6_000_000,
        14,
        grid=(NZ,),
        in_specs=[SMEM, whole((TOK, 2)), whole((TOK, 2)), whole(SLAB)],
        out_specs=[pl.BlockSpec((1, TOK, SHARD), lambda step: (step, 0, 0))] * 2,
        scratch_shapes=[ROW_SCRATCH, pltpu.VMEM((2, TOK, SLOTS), BF16)],
    )(place, codes, probs, returned)
    return keep.astype(F32) + swap(give, "core").astype(F32)


def combine(place, codes, probs, returned):
    early = lax.optimization_barrier(combine_chunk(0, place, codes, probs, returned[0]).astype(BF16))
    both = (combine_chunk(1, place, codes, probs, returned[1]) + early.astype(F32)).astype(BF16)
    total = lax.dynamic_index_in_dim(both, place[0], 0, False).astype(F32)
    for step in range(1, NZ):
        piece = lax.dynamic_index_in_dim(both, lax.rem(place[0] + step, NZ), 0, False)
        total = total + shift(piece, "z_hi", NZ, step).astype(F32)
    return total


def shards(
    attention,
    out_weight,
    residual,
    norm_gain,
    expert_ids,
    slot_index,
    gate_prob,
    w_gate,
    w_up,
    w_down,
):
    place = jnp.stack([lax.axis_index(name) for name in ("z_hi", "core", "z_lo", "x", "y")])
    place = place.astype(jnp.int32)
    slot = slot_index - SHARE * place[1]
    codes = jnp.where((slot_index >= 0) & (slot >= 0) & (slot < SHARE), 16 * expert_ids + slot, -1)

    hidden_state = project(place, attention, out_weight, residual)
    one, two = dispatch(place, codes.T, hidden_state, norm_gain)
    one, hidden_state, gate, up, down = lax.optimization_barrier(
        (one, hidden_state, w_gate[0], w_up[0], w_down[0])
    )
    gate, up, down = [(value, swap(value, "core")) for value in (gate, up, down)]
    two, gate, up, down = lax.optimization_barrier((two, gate, up, down))
    returned = []
    for rows in (one, two):
        arrived = lax.all_to_all(rows, EXPERT, split_axis=0, concat_axis=0, tiled=True)
        half_out = experts(arrived, gate, up, down)
        returned.append(lax.all_to_all(half_out, EXPERT, split_axis=0, concat_axis=0, tiled=True))
    expert_mix = combine(place, codes, gate_prob, returned)
    return (hidden_state + expert_mix).astype(BF16)


def solution(mesh):
    fine = Mesh(mesh.devices.reshape(SIZES), EXPERT + MP)
    return jax.shard_map(
        shards,
        mesh=fine,
        in_specs=(
            P(EXPERT, MP),
            P(EXPERT, MP),
            P(EXPERT, MP),
            P(MP),
            P(EXPERT, None),
            P(EXPERT, None),
            P(EXPERT, None),
            P(EXPERT, None, MP),
            P(EXPERT, None, MP),
            P(EXPERT, MP, None),
        ),
        out_specs=P(EXPERT, MP),
        check_vma=False,
    )
```
